256 devices in a mesh: dom: 64 (over z, x, core), feat: 4 (over y).
Axes of the slice: x: 4, y: 4, z: 8, core: 2. Of those that a mesh axis runs over, the one named last changes fastest.
Arguments:
- hidden: bfloat16 [256, 262144], P('feat', 'dom'), may hold values from -6 to 6
- tiles: bfloat16 [2048, 12, 128, 128], P('dom')
- tile_src: int32 [2048, 12], P('dom'), may hold values from 0 to 167, as said below
- hub_blocks: int32 [64, 2], P('dom'), may hold values from 0 to 31, as said below
- halo_rows: int32 [64, 64, 16], P('dom'), may hold values from 0 to 4095
- halo_counts: int32 [64, 64], replicated, may hold values from 0 to 16, as said below
- weight_self: bfloat16 [172, 256], P('feat'), may hold values from -0.375 to 0.375
- weight_neigh: bfloat16 [172, 256], P('feat'), may hold values from -0.75 to 0.75
- grad_logits: bfloat16 [172, 262144], P('feat', 'dom'), may hold values from -6 to 6
Outputs:
- logits: bfloat16 [172, 262144], P('feat', 'dom')
- grad_self: float32 [172, 256], P('feat', 'dom')
- grad_neigh: float32 [172, 256], P('feat', 'dom')
- grad_hidden: float32 [256, 262144], P('feat', 'dom')
The draws below stay inside these ranges and needn't reach their ends.
Inputs may be any that keep to these rules, and one draw needn't show every extreme that they name: `tile_src`: blocks below 32 are the partition's own nodes, the next 8 the received slots, the rest the hub blocks; the first tile of every destination block reads the partition's own nodes. `hub_blocks`: 2 distinct blocks a partition. `halo_counts`: zero where a partition meets itself, at least 1 elsewhere; in every draw some partition receives 16 live slots from every other partition. `halo_rows`: entries beyond the live count of a pair are padding.
All inputs are finite; a program needn't handle non-finite values.
Results may differ from the reference program's by a relative error of at most 0.0035.
Values may be sent and summed in bfloat16 or wider, within the bound.
A program may use at most 128 MiB of HBM per device.

```python
import jax
import jax.numpy as jnp
from jax import lax

H = 256
C = 172
BLK = 128
ROWS_DEV = 4096
TPB = 12
HB = 2
CAP = 16
NB = 32
NODES = 262144
HALO_BLK = 8
EXT = 168
N_DOM = 64


def draw_tiles(key, part):
    key = jax.random.fold_in(key, 17)
    key_major, key_minor, key_first, key_second = jax.random.split(key, 4)
    count = N_DOM * NB * TPB
    first_perm = jax.vmap(lambda k: jax.random.permutation(k, BLK))(jax.random.split(key_first, count))
    second_perm = jax.vmap(lambda k: jax.random.permutation(k, BLK))(jax.random.split(key_second, count))
    major = jnp.exp(jax.random.uniform(key_major, (count, BLK), jnp.float32, 0.0, 0.6931))
    minor = jax.random.uniform(key_minor, (count, BLK), jnp.float32, 0.4, 0.9)
    cols = jnp.arange(BLK, dtype=jnp.int32)
    tile_values = major[:, :, None] * (first_perm[:, :, None] == cols).astype(jnp.float32)
    tile_values = tile_values + minor[:, :, None] * (second_perm[:, :, None] == cols).astype(jnp.float32)
    return tile_values.reshape(N_DOM * NB, TPB, BLK, BLK).astype(jnp.bfloat16)


def draw_tile_src(key, part):
    key = jax.random.fold_in(key, 11)
    keys = jax.random.split(key, 6)
    count = N_DOM * NB
    kinds = jax.random.randint(keys[0], (count, TPB), 0, 3)
    own_block = jax.random.randint(keys[1], (count, TPB), 0, NB)
    halo_block = NB + jax.random.randint(keys[2], (count, TPB), 0, HALO_BLK)
    hub_block = NB + HALO_BLK + jax.random.randint(keys[3], (count, TPB), 0, N_DOM * HB)
    chosen = jnp.where(kinds == 0, own_block, jnp.where(kinds == 1, halo_block, hub_block))
    chosen = chosen.at[:, 0].set(own_block[:, 0])
    high_row = jax.random.randint(keys[4], (), 0, count)
    low_row = jax.random.randint(keys[5], (), 0, count)
    chosen = chosen.at[high_row, TPB - 1].set(EXT - 1)
    chosen = chosen.at[low_row, 0].set(0)
    return chosen.astype(jnp.int32)


def draw_hub_blocks(key, part):
    key = jax.random.fold_in(key, 23)
    picks = jax.vmap(lambda k: jax.random.permutation(k, NB)[:HB])(jax.random.split(key, N_DOM))
    return picks.astype(jnp.int32)


def draw_halo_counts(key, part):
    key = jax.random.fold_in(key, 29)
    key_counts, key_target = jax.random.split(key)
    counts = jax.random.randint(key_counts, (N_DOM, N_DOM), 1, CAP + 1)
    target = jax.random.randint(key_target, (), 0, N_DOM)
    index = jnp.arange(N_DOM, dtype=jnp.int32)
    counts = jnp.where(index[None, :] == target, CAP, counts)
    counts = jnp.where(index[:, None] == index[None, :], 0, counts)
    return counts.astype(jnp.int32)


def touch_ends(result, stream_key, smallest, top_value):
    index_at = [jax.random.randint(jax.random.fold_in(stream_key, axis), (), 0, length) for axis, length in enumerate(result.shape)]
    main_axis = result.shape.index(max(result.shape))
    neighbour = index_at[:main_axis] + [(index_at[main_axis] + 1) % result.shape[main_axis]] + index_at[main_axis + 1:]
    return result.at[tuple(index_at)].set(smallest).at[tuple(neighbour)].set(top_value)


def steps_of(own_key, extent, pieces, least, largest):
    def one(dim, parts):
        heights = jax.random.uniform(jax.random.fold_in(jax.random.fold_in(own_key, 6), dim), (parts,), jnp.float32, least / len(pieces), largest / len(pieces))
        return jnp.repeat(jnp.exp(heights), extent[dim] // parts).reshape((-1,) + (1,) * (len(extent) - dim - 1))

    loudness = one(*pieces[0])
    for cut in pieces[1:]:
        loudness = loudness * one(*cut)
    return loudness


def noise(stream_key, extent, scale, most, cuts=(), kind=jnp.bfloat16):
    entries = jax.random.normal(stream_key, extent, jnp.float32) * scale
    if len(cuts) > 0:
        entries = steps_of(stream_key, extent, cuts, -0.22, 0.18) * entries
    return jnp.clip(entries, min=-most, max=most).astype(kind)


def setup_inputs(seed: int = 0) -> dict:
    key_list = jax.random.split(jax.random.key(seed), 10)
    return {
        "hidden": noise(key_list[0], (H, NODES), 1.0, 6.0, ((0, 4), (1, 64))),
        "tiles": draw_tiles(jax.random.fold_in(key_list[9], 71), 0),
        "tile_src": draw_tile_src(jax.random.fold_in(key_list[9], 71), 0),
        "hub_blocks": draw_hub_blocks(jax.random.fold_in(key_list[9], 71), 0),
        "halo_rows": touch_ends(jax.random.randint(key_list[4], (N_DOM, N_DOM, CAP), 0, ROWS_DEV), jax.random.fold_in(key_list[4], 1), 0, ROWS_DEV - 1).astype(jnp.int32),
        "halo_counts": draw_halo_counts(jax.random.fold_in(key_list[9], 71), 0),
        "weight_self": noise(key_list[6], (C, H), H ** -0.5, 0.375, ((0, 4),)),
        "weight_neigh": noise(key_list[7], (C, H), (H // 4) ** -0.5, 0.75, ((0, 4),)),
        "grad_logits": noise(key_list[8], (C, NODES), 1.0, 6.0, ((0, 4), (1, 64))),
    }


def reference(hidden, tiles, tile_src, hub_blocks, halo_rows, halo_counts, weight_self, weight_neigh, grad_logits):
    part_base = jnp.arange(N_DOM, dtype=jnp.int32) * ROWS_DEV
    within = jnp.arange(BLK, dtype=jnp.int32)
    hub_index = ((part_base[:, None] + hub_blocks * BLK)[:, :, None] + within[None, None, :]).reshape(-1).astype(jnp.int32)
    hub_table = jnp.take(hidden, hub_index, axis=1)
    alive_all = (jnp.arange(CAP, dtype=jnp.int32)[None, None, :] < halo_counts[:, :, None]).astype(jnp.float32)
    halo_index = (part_base[:, None, None] + halo_rows).astype(jnp.int32)
    tile_parts = tiles.reshape(N_DOM, NB, TPB, BLK, BLK)
    source_parts = tile_src.reshape(N_DOM, NB, TPB)
    ones_own = jnp.ones((ROWS_DEV,), jnp.float32)
    ones_hubs = jnp.ones((N_DOM * HB * BLK,), jnp.float32)

    def part_tables(part_id):
        alive_slots = jnp.take(alive_all, part_id, axis=1)
        live_table = jnp.concatenate([ones_own, alive_slots.reshape(-1), ones_hubs]).reshape(EXT, BLK)
        sources = jnp.take(source_parts, part_id, axis=0).reshape(-1)
        weights = jnp.take(tile_parts, part_id, axis=0).astype(jnp.float32)
        senders = jnp.take(halo_index, part_id, axis=1).reshape(-1)
        return alive_slots, live_table, sources, weights, senders

    def forward_part(part_id):
        alive_slots, live_table, sources, weights, senders = part_tables(part_id)
        own_rows = lax.dynamic_slice_in_dim(hidden, part_id * ROWS_DEV, ROWS_DEV, 1)
        halo_part = jnp.take(hidden, senders, axis=1) * alive_slots.reshape(-1).astype(hidden.dtype)
        sources_table = jnp.concatenate([own_rows, halo_part, hub_table], axis=1).reshape(H, EXT, BLK)
        picked = jnp.take(sources_table, sources, axis=1).reshape(H, NB, TPB, BLK).astype(jnp.float32)
        summed = jnp.einsum('bjds,cbjs->cbd', weights, picked)
        live_tiles = jnp.take(live_table, sources, axis=0).reshape(NB, TPB, BLK)
        degree = jnp.einsum('bjds,bjs->bd', weights, live_tiles)
        averaged = (summed / degree[None]).reshape(H, ROWS_DEV).astype(jnp.bfloat16)
        return averaged, degree.reshape(ROWS_DEV)

    averages, degrees = lax.map(forward_part, jnp.arange(N_DOM, dtype=jnp.int32))
    neighbours = jnp.moveaxis(averages, 0, 1).reshape(H, NODES)
    degree_all = degrees.reshape(NODES)
    logits = (jnp.dot(weight_self, hidden, preferred_element_type=jnp.float32)
              + jnp.dot(weight_neigh, neighbours, preferred_element_type=jnp.float32)).astype(jnp.bfloat16)
    factor = float(NODES) ** -0.5
    grad_self = jnp.dot(grad_logits, hidden.T, preferred_element_type=jnp.float32) * factor
    grad_neigh = jnp.dot(grad_logits, neighbours.T, preferred_element_type=jnp.float32) * factor
    direct = jnp.dot(weight_self.T, grad_logits, preferred_element_type=jnp.float32)
    spread = jnp.dot(weight_neigh.T, grad_logits, preferred_element_type=jnp.float32)
    scaled = (spread / degree_all[None]).astype(jnp.bfloat16)

    def backward_part(running, part_id):
        alive_slots, live_table, sources, weights, senders = part_tables(part_id)
        offset = part_id * ROWS_DEV
        upstream = lax.dynamic_slice_in_dim(scaled, offset, ROWS_DEV, 1).reshape(H, NB, BLK).astype(jnp.float32)
        pushed = jnp.einsum('bjds,cbd->cbjs', weights, upstream).reshape(H, NB * TPB, BLK)
        returned = jnp.zeros((H, EXT, BLK), jnp.float32).at[:, sources].add(pushed) * live_table[None]
        flattened = returned.reshape(H, EXT * BLK)
        updated = lax.dynamic_slice_in_dim(running, offset, ROWS_DEV, 1) + flattened[:, :ROWS_DEV]
        running = lax.dynamic_update_slice_in_dim(running, updated, offset, 1)
        running = running.at[:, senders].add(flattened[:, ROWS_DEV:ROWS_DEV + N_DOM * CAP])
        running = running.at[:, hub_index].add(flattened[:, ROWS_DEV + N_DOM * CAP:])
        return running, None

    grad_hidden, unused = lax.scan(backward_part, direct, jnp.arange(N_DOM, dtype=jnp.int32))
    return logits, grad_self, grad_neigh, grad_hidden
```

```python
import jax
import jax.numpy as jnp
from jax import lax
from jax.experimental import pallas as pl
from jax.experimental.pallas import tpu as pltpu
from jax.sharding import PartitionSpec as P

BF = jnp.bfloat16
F32 = jnp.float32
BLK = 128
ROWS_DEV = 4096
TPB = 12
HB = 2
CAP = 16
NB = 32
NZ, NX, NC, NF = 8, 4, 2, 4
PARTS = NZ * NX * NC
GR = 43
GP = 48
FD = 64
EXT = 168
TR = 80
VM = pltpu.VMEM
CHUNK = 512
NT = (((1,), (1,)), ((), ()))
TN = (((0,), (0,)), ((), ()))


def spec(space=pltpu.VMEM):
    return pl.BlockSpec(memory_space=space)


def one_hot_rows(rows, start, size):
    node = lax.broadcasted_iota(jnp.int32, (size, PARTS * CAP), 0) + start
    return (node == rows).astype(F32).astype(BF)


def prep_kernel(hub_ref, hidden_ref, rows_ref, halo_ref, hubs_ref, total):
    core = lax.rem(lax.axis_index("dom"), NC)
    for i in range(HB):
        start = pl.multiple_of(hub_ref[0, i] * BLK, BLK)
        hubs_ref[i] = hidden_ref[:, pl.ds(start, BLK)]
    rows = rows_ref[...]
    total[...] = jnp.zeros_like(total)

    @pl.loop(0, ROWS_DEV // CHUNK)
    def _(i):
        start = pl.multiple_of(i * CHUNK, CHUNK)
        hot = one_hot_rows(rows, start, CHUNK)
        total[...] += jnp.dot(hidden_ref[:, pl.ds(start, CHUNK)], hot, preferred_element_type=F32)

    for k in range(NZ):
        piece = total[:, k * BLK : (k + 1) * BLK]
        zero = jnp.zeros_like(piece)
        both = jnp.concatenate(
            [jnp.where(core == 0, piece, zero), jnp.where(core == 1, piece, zero)], axis=0
        )
        halo_ref[k] = both.T.astype(BF).reshape(NX, NC, CAP, BLK)


def prep(hub_blocks, hidden, rows):
    return pl.pallas_call(
        prep_kernel,
        out_shape=(
            jax.ShapeDtypeStruct((NZ, NX, NC, CAP, BLK), BF),
            jax.ShapeDtypeStruct((HB, FD, BLK), BF),
        ),
        in_specs=[spec(pltpu.SMEM), spec(), spec()],
        out_specs=(spec(), spec()),
        scratch_shapes=[VM((FD, PARTS * CAP), F32)],
        compiler_params=pltpu.CompilerParams(vmem_limit_bytes=32 << 20),
    )(hub_blocks, hidden, rows)


def slot_place():
    row = lax.broadcasted_iota(jnp.int32, (NX * CAP, NC * BLK), 0)
    lane = lax.broadcasted_iota(jnp.int32, (NX * CAP, NC * BLK), 1)
    want = (row // CAP) * (NC * CAP) + (lane // BLK) * CAP + row % CAP
    return (lane % BLK == want).astype(F32).astype(BF)


def layer_kernel(
    src_ref,
    tiles_ref,
    hidden_ref,
    halo_ref,
    hubs_ref,
    counts_ref,
    gl_ref,
    w_ref,
    own_ref,
    back_ref,
    hubg_ref,
    part_ref,
    mine_ref,
    pg_ref,
    table,
    live,
    acc,
    wt,
    logit,
    grads,
):
    step = pl.program_id(0)
    dom = lax.axis_index("dom")
    feat = lax.axis_index("feat")

    @pl.when(step == 0)
    def _():
        acc[...] = jnp.zeros_like(acc)
        grads[...] = jnp.zeros_like(grads)
        wt[...] = w_ref[...].reshape(NF * GP, 2 * FD).astype(F32).T.astype(BF)
        rows = TR - FD
        first = (lax.broadcasted_iota(jnp.int32, (rows, BLK), 0) == 0).astype(F32)
        ones = first.astype(BF)
        pick = (lax.broadcasted_iota(jnp.int32, (16, PARTS), 1) == dom).astype(F32).astype(BF)
        got = lax.dot_general(
            pick, counts_ref[...].astype(F32).astype(BF), NT, preferred_element_type=F32
        )
        sender = lax.broadcasted_iota(jnp.int32, (PARTS, PARTS * CAP), 0)
        column = lax.broadcasted_iota(jnp.int32, (PARTS, PARTS * CAP), 1)
        spread_out = (column // CAP == sender).astype(F32).astype(BF)
        limit = jnp.dot(got.astype(BF), spread_out, preferred_element_type=F32)
        slot = lax.broadcasted_iota(jnp.int32, (16, PARTS * CAP), 1) % CAP
        live[...] = (slot.astype(F32) < limit).astype(F32)
        for b in range(NB):
            table[b, 0:FD] = hidden_ref[:, b * BLK : (b + 1) * BLK]
            table[b, FD:TR] = ones
        place = slot_place()
        for z in range(NZ):
            rows_z = halo_ref[:, z].reshape(NX * CAP, BLK)
            res = lax.dot_general(rows_z, place, TN, preferred_element_type=F32)
            alive = live[0:1, z * BLK : (z + 1) * BLK]
            block = (res[0:FD, 0:BLK] + res[FD:, BLK:]) * alive
            table[NB + z, 0:FD] = block.astype(BF)
            table[NB + z, FD:TR] = (first * alive).astype(BF)

        @pl.loop(0, PARTS * HB)
        def _(h):
            table[NB + NZ + h, 0:FD] = hubs_ref[h]
            table[NB + NZ + h, FD:TR] = ones

    span = pl.ds(pl.multiple_of(step * (2 * BLK), 2 * BLK), 2 * BLK)
    gl = gl_ref[:, :, span].reshape(NF * GP, 2 * BLK)
    both = jnp.dot(wt[...], gl, preferred_element_type=F32)
    means = []
    for k in range(2):
        b = step * 2 + k
        picks = [src_ref[b, j] for j in range(TPB)]
        weights = jnp.concatenate([tiles_ref[k, j] for j in range(TPB)], axis=1)
        picked = jnp.concatenate([table[picks[j]] for j in range(TPB)], axis=1)
        summed = lax.dot_general(picked, weights, NT, preferred_element_type=F32)
        degree = summed[FD : FD + 1]
        means.append((summed[0:FD] / degree).astype(BF))
        lanes = slice(k * BLK, (k + 1) * BLK)
        scaled = (both[FD:, lanes] / degree).astype(BF)
        acc[b] += both[0:FD, lanes]
        pushed = jnp.dot(scaled, weights, preferred_element_type=F32)
        for j in range(TPB):
            acc[picks[j]] += pushed[:, j * BLK : (j + 1) * BLK]
    x = jnp.concatenate([hidden_ref[:, span], jnp.concatenate(means, axis=1)], axis=0)
    logit[...] = jnp.dot(
        w_ref[...].reshape(NF * GP, 2 * FD), x, preferred_element_type=F32
    ).reshape(NF, GP, 2 * BLK)
    part_ref[:, :, span] = logit[...].astype(BF)
    mine_ref[:, span] = logit[feat]
    grads[...] += lax.dot_general(x, gl, NT, preferred_element_type=F32)

    @pl.when(step == NB // 2 - 1)
    def _():
        for b in range(NB):
            own_ref[:, b * BLK : (b + 1) * BLK] = acc[b]
        place = slot_place()
        for z in range(NZ):
            block = (acc[NB + z] * live[0:1, z * BLK : (z + 1) * BLK]).astype(BF)
            zero = jnp.zeros_like(block)
            wide = jnp.concatenate(
                [jnp.concatenate([block, zero], axis=1), jnp.concatenate([zero, block], axis=1)],
                axis=0,
            )
            back = lax.dot_general(place, wide, NT, preferred_element_type=F32)
            back_ref[:, z] = back.astype(BF).reshape(NX, CAP, BLK)

        @pl.loop(0, PARTS * HB)
        def _(h):
            hubg_ref[h] = acc[NB + NZ + h].astype(BF)

        total = grads[...] * float(PARTS * ROWS_DEV) ** (-0.5)
        for j in range(16):
            pair = jnp.concatenate([total[4 * j : 4 * j + 4], total[FD + 4 * j : FD + 4 * j + 4]], axis=0)
            for f in range(NF):
                pg_ref[f, j] = jnp.concatenate(
                    [pair[:, f * GP : (f + 1) * GP], jnp.zeros((8, BLK - GP), F32)], axis=1
                )


def layer(src, tiles, hidden, halo, hubs, counts, gl, w):
    outs = (
        jax.ShapeDtypeStruct((FD, ROWS_DEV), F32),
        jax.ShapeDtypeStruct((NX, NZ, CAP, BLK), BF),
        jax.ShapeDtypeStruct((PARTS * HB, FD, BLK), BF),
        jax.ShapeDtypeStruct((NF, GP, ROWS_DEV), BF),
        jax.ShapeDtypeStruct((GP, ROWS_DEV), F32),
        jax.ShapeDtypeStruct((NF, 16, 8, BLK), F32),
    )
    return pl.pallas_call(
        layer_kernel,
        grid=(NB // 2,),
        out_shape=outs,
        in_specs=[
            spec(pltpu.SMEM),
            pl.BlockSpec((2, TPB, BLK, BLK), lambda i: (i, 0, 0, 0)),
        ]
        + [spec()] * 6,
        out_specs=(spec(),) * 6,
        scratch_shapes=[
            VM((EXT, TR, BLK), BF),
            VM((16, PARTS * CAP), F32),
            VM((EXT, FD, BLK), F32),
            VM((2 * FD, NF * GP), BF),
            VM((NF, GP, 2 * BLK), F32),
            VM((2 * FD, NF * GP), F32),
        ],
        compiler_params=pltpu.CompilerParams(vmem_limit_bytes=56 << 20),
    )(src, tiles, hidden, halo, hubs, counts, gl, w)


def finish_kernel(hub_ref, own_ref, rows_ref, first_ref, second_ref, sum_ref, out_ref):
    core = lax.rem(lax.axis_index("dom"), NC)
    flat = []
    for k in range(NZ * NX // 4):
        a = first_ref[pl.ds(4 * k, 4)]
        b = second_ref[pl.ds(4 * k, 4)]
        turned = jnp.stack([a, b], axis=1).reshape(BLK, BLK).astype(F32).T
        flat.append(jnp.where(core == 0, turned[0:FD], turned[FD:]).astype(BF))
    back = jnp.concatenate(flat, axis=1)
    rows = rows_ref[...]

    @pl.loop(0, ROWS_DEV // CHUNK)
    def _(i):
        start = pl.multiple_of(i * CHUNK, CHUNK)
        hot = one_hot_rows(rows, start, CHUNK)
        got = lax.dot_general(back, hot, NT, preferred_element_type=F32)
        out_ref[:, pl.ds(start, CHUNK)] = own_ref[:, pl.ds(start, CHUNK)] + got

    for i in range(HB):
        start = pl.multiple_of(hub_ref[0, i] * BLK, BLK)
        out_ref[:, pl.ds(start, BLK)] += sum_ref[i]


def finish(hub_blocks, own, rows, first, second, hub_sum):
    return pl.pallas_call(
        finish_kernel,
        out_shape=jax.ShapeDtypeStruct((FD, ROWS_DEV), F32),
        in_specs=[spec(pltpu.SMEM)] + [spec()] * 5,
        out_specs=spec(),
        compiler_params=pltpu.CompilerParams(vmem_limit_bytes=32 << 20),
    )(hub_blocks, own, rows, first, second, hub_sum)


def local(
    hidden,
    tiles,
    tile_src,
    hub_blocks,
    halo_rows,
    halo_counts,
    weight_self,
    weight_neigh,
    grad_logits,
):
    rows = halo_rows.reshape(1, PARTS * CAP)
    halo_out, hub_piece = prep(hub_blocks, hidden, rows)
    pad = ((0, GP - GR), (0, 0))
    hubs = lax.all_gather(hub_piece, "dom", axis=0, tiled=True)
    gl = lax.all_gather(jnp.pad(grad_logits, pad), "feat", axis=0, tiled=False)
    w = jnp.stack(
        [weight_self.reshape(GR, NF, FD), weight_neigh.reshape(GR, NF, FD)], axis=2
    ).reshape(GR, NF, 2 * FD)
    w = jnp.pad(w.transpose(1, 0, 2), ((0, 0), (0, GP - GR), (0, 0)))
    w = lax.all_to_all(w, "feat", 0, 0, tiled=True)
    halo = lax.all_to_all(halo_out.reshape(PARTS, CAP, BLK), "dom", 0, 0, tiled=True)
    halo = halo.reshape(NZ, NX, NC, CAP, BLK).sum(axis=2).transpose(1, 0, 2, 3)
    own, back, hubg, part, mine, pg = layer(
        tile_src, tiles, hidden, halo, hubs, halo_counts, gl, w
    )
    parts = lax.all_to_all(part, "feat", 0, 0, tiled=True)
    feat = lax.axis_index("feat")
    others = jnp.arange(NF)[:, None, None] != feat
    logits = (mine + jnp.where(others, parts.astype(F32), 0.0).sum(axis=0))[:GR].astype(BF)
    hub_sum = lax.psum_scatter(hubg.astype(F32), "dom", scatter_dimension=0, tiled=True)
    pg = lax.psum_scatter(pg.reshape(PARTS, 8, BLK), "dom", scatter_dimension=0, tiled=True)[0]
    moves = [
        ((16 * g + j) * NF + f, (16 * f + j) * NF + g)
        for g in range(NF)
        for j in range(16)
        for f in range(NF)
    ]
    pg = lax.ppermute(pg, ("dom", "feat"), moves)
    grad_self, grad_neigh = pg[:4, :GR].T, pg[4:, :GR].T
    back = jnp.broadcast_to(back.transpose(1, 0, 2, 3)[:, :, None], (NZ, NX, NC, CAP, BLK))
    back = lax.all_to_all(back.reshape(PARTS, CAP, BLK), "dom", 0, 0, tiled=True)
    back = back.reshape(NZ * NX, NC, CAP, BLK)
    grad_hidden = finish(hub_blocks, own, rows, back[:, 0], back[:, 1], hub_sum)
    return logits, grad_self, grad_neigh, grad_hidden


def solution(mesh):
    placed = (
        P("feat", "dom"),
        P("dom", None, None, None),
        P("dom", None),
        P("dom", None),
        P("dom", None, None),
        P(),
        P("feat", None),
        P("feat", None),
        P("feat", "dom"),
    )
    return jax.shard_map(
        local,
        mesh=mesh,
        in_specs=placed,
        out_specs=(P("feat", "dom"), P("feat", "dom"), P("feat", "dom"), P("feat", "dom")),
        check_vma=False,
    )
```

```python
import jax
import jax.numpy as jnp
from jax import lax
from jax.experimental import pallas as pl
from jax.experimental.pallas import tpu as pltpu
from jax.sharding import PartitionSpec as P

BF = jnp.bfloat16
F32 = jnp.float32
BLK = 128
ROWS_DEV = 4096
TPB = 12
HB = 2
CAP = 16
NB = 32
NZ, NX, NC, NF = 8, 4, 2, 4
PARTS = NZ * NX * NC
GR = 43
GP = 48
FD = 64
EXT = 168
TR = 80
VM = pltpu.VMEM
CHUNK = 512
NT = (((1,), (1,)), ((), ()))
TN = (((0,), (0,)), ((), ()))


def spec(space=pltpu.VMEM):
    return pl.BlockSpec(memory_space=space)


def one_hot_rows(rows, start, size):
    node = lax.broadcasted_iota(jnp.int32, (size, PARTS * CAP), 0) + start
    return (node == rows).astype(F32).astype(BF)


def place():
    dom = lax.axis_index("dom")
    return dom // (NX * NC), lax.rem(dom // NC, NX), lax.rem(dom, NC), lax.axis_index("feat")


def device(z, x, c, f):
    return ((lax.rem(z, NZ) * NX + lax.rem(x, NX)) * NC + c, lax.rem(f, NF))


def remote(src, dst, send, recv, target):
    return pltpu.make_async_remote_copy(
        src_ref=src,
        dst_ref=dst,
        send_sem=send,
        recv_sem=recv,
        device_id=target,
        device_id_type=pl.DeviceIdType.MESH,
    )


def meet(targets):
    barrier = pltpu.get_barrier_semaphore()
    for target in targets:
        pl.semaphore_signal(
            barrier, inc=1, device_id=target, device_id_type=pl.DeviceIdType.MESH
        )
    return barrier


HALF = ROWS_DEV // 2


def gather_kernel(
    hub_ref,
    hidden_ref,
    rows_ref,
    gl_in,
    ws_ref,
    wn_ref,
    gl_ref,
    w_ref,
    hubs_ref,
    halo_ref,
    wsend,
    total,
    outgoing,
    sibling,
    merged,
    planes,
    y_send,
    y_recv,
    w_send,
    w_recv,
    hx_send,
    hx_recv,
    hz_send,
    hz_recv,
    hc_send,
    hc_recv,
    c_send,
    c_recv,
    z_send,
    z_recv,
    x_send,
    x_recv,
):
    z, x, c, f = place()
    pair = device(z, x, 1 - c, f)
    barrier = meet(
        [device(z, x, c, f + o) for o in range(1, NF)]
        + [device(z + o, x, c, f) for o in range(1, NZ)]
        + [device(z, x + o, c, f) for o in range(1, NX)]
        + [pair]
    )

    gl_ref[f, 32:GP, :] = jnp.zeros((GP - 32, ROWS_DEV), BF)
    gl_ref[f, 0:GR, :] = gl_in[...]
    for g in range(NF):
        wsend[g] = jnp.zeros((GP, 2 * FD), BF)
        cols = slice(g * FD, (g + 1) * FD)
        wsend[g, 0:GR] = jnp.concatenate([ws_ref[:, cols], wn_ref[:, cols]], axis=1)
    w_ref[f] = wsend[f]
    for i in range(HB):
        wanted = hub_ref[0, i]
        piece = hidden_ref[:, 0:BLK]
        for b in range(1, NB):
            piece = jnp.where(wanted == b, hidden_ref[:, b * BLK : (b + 1) * BLK], piece)
        hubs_ref[z, x, c, i] = piece
    pl.semaphore_wait(barrier, NF + NZ + NX - 2)

    def y_copy(way, k, origin, half):
        part = gl_ref.at[lax.rem(origin + NF, NF), :, pl.ds(half * HALF, HALF)]
        target = device(z, x, c, f + (1 if way == 0 else NF - 1))
        return remote(part, part, y_send.at[way, k], y_recv.at[way, k], target)

    y_first = [y_copy(0, 0, f, 0), y_copy(1, 0, f, 1), y_copy(0, 1, f, 1), y_copy(1, 1, f, 0)]
    for copy in y_first:
        copy.start()

    hx = [
        remote(
            hubs_ref.at[z, x, c],
            hubs_ref.at[z, x, c],
            hx_send.at[o - 1],
            hx_recv.at[o - 1],
            device(z, x + o, c, f),
        )
        for o in range(1, NX)
    ]
    for copy in hx:
        copy.start()
    ws = [
        remote(
            wsend.at[lax.rem(f + o, NF)],
            w_ref.at[f],
            w_send.at[o - 1],
            w_recv.at[o - 1],
            device(z, x, c, f + o),
        )
        for o in range(1, NF)
    ]
    for copy in ws:
        copy.start()

    def hz_copy(way, k, half):
        origin = lax.rem(z + (NZ - k if way == 0 else k), NZ)
        part = hubs_ref.at[origin, pl.ds(2 * half, 2), c]
        target = device(z + (1 if way == 0 else NZ - 1), x, c, f)
        return remote(part, part, hz_send.at[way, k, half], hz_recv.at[way, k, half], target)

    def hc_copy(k, half):
        part = hubs_ref.at[lax.rem(z + k, NZ), pl.ds(2 * half, 2), c]
        return remote(part, part, hc_send.at[k, half], hc_recv.at[k, half], pair)

    def hc_recv_wait(k, half):
        part = hubs_ref.at[lax.rem(z + k, NZ), pl.ds(2 * half, 2), 1 - c]
        remote(part, part, hc_send.at[k, half], hc_recv.at[k, half], pair).wait_recv()

    def hz_wait(way, k, half):
        origin = lax.rem(z + (NZ - k - 1 if way == 0 else k + 1), NZ)
        part = hubs_ref.at[origin, pl.ds(2 * half, 2), c]
        remote(part, part, hz_send.at[way, k, half], hz_recv.at[way, k, half], pair).wait_recv()

    sent = []

    def go(copy):
        copy.start()
        sent.append(copy)

    rows = rows_ref[...]
    total[...] = jnp.zeros_like(total)

    def gather(first, last):
        @pl.loop(first, last)
        def _(i):
            start = pl.multiple_of(i * CHUNK, CHUNK)
            hot = one_hot_rows(rows, start, CHUNK)
            total[...] += jnp.dot(
                hidden_ref[:, pl.ds(start, CHUNK)], hot, preferred_element_type=F32
            )

    gather(0, 3)
    for o in range(1, NX):
        part = hubs_ref.at[z, lax.rem(x + NX - o, NX), c]
        remote(part, part, hx_send.at[o - 1], hx_recv.at[o - 1], pair).wait_recv()
    for half in (0, 1):
        go(hz_copy(0, 0, half))
        go(hz_copy(1, 0, 1 - half))
    for half in (0, 1):
        go(hc_copy(0, half))
    gather(3, ROWS_DEV // CHUNK)
    for k in range(NZ):
        piece = total[:, k * BLK : (k + 1) * BLK]
        zero = jnp.zeros_like(piece)
        both = jnp.concatenate(
            [jnp.where(c == 0, piece, zero), jnp.where(c == 1, piece, zero)], axis=0
        )
        outgoing[k] = both.T.astype(BF).reshape(NX, NC, CAP, BLK)
    to_pair = remote(outgoing.at[:, :, 1 - c], sibling, c_send, c_recv, pair)
    go(to_pair)

    def y_wait(way, k, distance, half):
        origin = lax.rem(f + (NF - distance if way == 0 else distance), NF)
        part = gl_ref.at[origin, :, pl.ds(half * HALF, HALF)]
        remote(part, part, y_send.at[way, k], y_recv.at[way, k], pair).wait_recv()

    def ring(k):
        for half in (0, 1):
            for way in (0, 1):
                part = half if way == 0 else 1 - half
                if k == 3 and part != way:
                    continue
                hz_wait(way, k, part)
                if k < 2 or (k == 2 and part == way):
                    go(hz_copy(way, k + 1, part))
                go(hc_copy(NZ - k - 1 if way == 0 else k + 1, part))

    y_wait(0, 0, 1, 0)
    go(y_copy(0, 2, f - 1, 0))
    y_wait(1, 0, 1, 1)
    go(y_copy(1, 2, f + 1, 1))
    to_pair.wait_recv()
    merged[...] = outgoing[:, :, c] + sibling[...]
    for o in range(1, NZ):
        go(
            remote(
                merged.at[lax.rem(z + o, NZ)],
                planes.at[z],
                z_send.at[o - 1],
                z_recv.at[o - 1],
                device(z + o, x, c, f),
            )
        )
    planes[z] = merged[z]
    ring(0)
    for o in range(1, NZ):
        part = planes.at[lax.rem(z + NZ - o, NZ)]
        remote(part, part, z_send.at[o - 1], z_recv.at[o - 1], pair).wait_recv()
    for o in range(1, NX):
        go(
            remote(
                planes.at[:, lax.rem(x + o, NX)],
                halo_ref.at[x],
                x_send.at[o - 1],
                x_recv.at[o - 1],
                device(z, x + o, c, f),
            )
        )
    halo_ref[x] = planes[:, x]
    ring(1)
    for o in range(1, NX):
        part = halo_ref.at[lax.rem(x + NX - o, NX)]
        remote(part, part, x_send.at[o - 1], x_recv.at[o - 1], pair).wait_recv()
    ring(2)
    ring(3)
    for o in range(1, NF):
        part = w_ref.at[lax.rem(f + NF - o, NF)]
        remote(part, part, w_send.at[o - 1], w_recv.at[o - 1], pair).wait_recv()
    y_wait(0, 1, 1, 1)
    y_wait(1, 1, 1, 0)
    y_wait(0, 2, 2, 0)
    y_wait(1, 2, 2, 1)
    for k in range(NZ):
        for half in (0, 1):
            hc_recv_wait(k, half)
    for copy in y_first + hx + ws + sent:
        copy.wait_send()


def gather_all(hub_blocks, hidden, rows, grad_logits, weight_self, weight_neigh):
    dma = pltpu.SemaphoreType.DMA
    outs = (
        jax.ShapeDtypeStruct((NF, GP, ROWS_DEV), BF),
        jax.ShapeDtypeStruct((NF, GP, 2 * FD), BF),
        jax.ShapeDtypeStruct((NZ, NX, NC, HB, FD, BLK), BF),
        jax.ShapeDtypeStruct((NX, NZ, CAP, BLK), BF),
    )
    return pl.pallas_call(
        gather_kernel,
        out_shape=outs,
        in_specs=[spec(pltpu.SMEM)] + [spec()] * 5,
        out_specs=(spec(),) * 4,
        scratch_shapes=[
            VM((NF, GP, 2 * FD), BF),
            VM((FD, PARTS * CAP), F32),
            VM((NZ, NX, NC, CAP, BLK), BF),
            VM((NZ, NX, CAP, BLK), BF),
            VM((NZ, NX, CAP, BLK), BF),
            VM((NZ, NX, CAP, BLK), BF),
            dma((2, 3)),
            dma((2, 3)),
            dma((3,)),
            dma((3,)),
            dma((3,)),
            dma((3,)),
            dma((2, 4, 2)),
            dma((2, 4, 2)),
            dma((8, 2)),
            dma((8, 2)),
            dma,
            dma,
            dma((7,)),
            dma((7,)),
            dma((3,)),
            dma((3,)),
        ],
        compiler_params=pltpu.CompilerParams(
            collective_id=0, has_side_effects=True, vmem_limit_bytes=40 << 20
        ),
    )(hub_blocks, hidden, rows, grad_logits, weight_self, weight_neigh)


def slot_place():
    row = lax.broadcasted_iota(jnp.int32, (NX * CAP, NC * BLK), 0)
    lane = lax.broadcasted_iota(jnp.int32, (NX * CAP, NC * BLK), 1)
    want = (row // CAP) * (NC * CAP) + (lane // BLK) * CAP + row % CAP
    return (lane % BLK == want).astype(F32).astype(BF)


def layer_kernel(
    src_ref,
    tiles_ref,
    hidden_ref,
    halo_ref,
    hubs_ref,
    counts_ref,
    gl_ref,
    w_ref,
    own_ref,
    back_ref,
    hubg_ref,
    part_ref,
    mine_ref,
    pg_ref,
    table,
    live,
    acc,
    wt,
    logit,
    grads,
):
    step = pl.program_id(0)
    dom = lax.axis_index("dom")
    feat = lax.axis_index("feat")

    @pl.when(step == 0)
    def _():
        acc[...] = jnp.zeros_like(acc)
        grads[...] = jnp.zeros_like(grads)
        wt[...] = w_ref[...].reshape(NF * GP, 2 * FD).astype(F32).T.astype(BF)
        rows = TR - FD
        first = (lax.broadcasted_iota(jnp.int32, (rows, BLK), 0) == 0).astype(F32)
        ones = first.astype(BF)
        pick = (lax.broadcasted_iota(jnp.int32, (16, PARTS), 1) == dom).astype(F32).astype(BF)
        got = lax.dot_general(
            pick, counts_ref[...].astype(F32).astype(BF), NT, preferred_element_type=F32
        )
        sender = lax.broadcasted_iota(jnp.int32, (PARTS, PARTS * CAP), 0)
        column = lax.broadcasted_iota(jnp.int32, (PARTS, PARTS * CAP), 1)
        spread_out = (column // CAP == sender).astype(F32).astype(BF)
        limit = jnp.dot(got.astype(BF), spread_out, preferred_element_type=F32)
        slot = lax.broadcasted_iota(jnp.int32, (16, PARTS * CAP), 1) % CAP
        live[...] = (slot.astype(F32) < limit).astype(F32)
        for b in range(NB):
            table[b, 0:FD] = hidden_ref[:, b * BLK : (b + 1) * BLK]
            table[b, FD:TR] = ones
        place = slot_place()
        for z in range(NZ):
            rows_z = halo_ref[:, z].reshape(NX * CAP, BLK)
            res = lax.dot_general(rows_z, place, TN, preferred_element_type=F32)
            alive = live[0:1, z * BLK : (z + 1) * BLK]
            block = (res[0:FD, 0:BLK] + res[FD:, BLK:]) * alive
            table[NB + z, 0:FD] = block.astype(BF)
            table[NB + z, FD:TR] = (first * alive).astype(BF)

        @pl.loop(0, PARTS * HB)
        def _(h):
            table[NB + NZ + h, 0:FD] = hubs_ref[h]
            table[NB + NZ + h, FD:TR] = ones

    span = pl.ds(pl.multiple_of(step * (2 * BLK), 2 * BLK), 2 * BLK)
    gl = gl_ref[:, :, span].reshape(NF * GP, 2 * BLK)
    both = jnp.dot(wt[...], gl, preferred_element_type=F32)
    means = []
    for k in range(2):
        b = step * 2 + k
        picks = [src_ref[b, j] for j in range(TPB)]
        weights = jnp.concatenate([tiles_ref[k, j] for j in range(TPB)], axis=1)
        picked = jnp.concatenate([table[picks[j]] for j in range(TPB)], axis=1)
        summed = lax.dot_general(picked, weights, NT, preferred_element_type=F32)
        degree = summed[FD : FD + 1]
        means.append((summed[0:FD] / degree).astype(BF))
        lanes = slice(k * BLK, (k + 1) * BLK)
        scaled = (both[FD:, lanes] / degree).astype(BF)
        acc[b] += both[0:FD, lanes]
        pushed = jnp.dot(scaled, weights, preferred_element_type=F32)
        for j in range(TPB):
            acc[picks[j]] += pushed[:, j * BLK : (j + 1) * BLK]
    x = jnp.concatenate([hidden_ref[:, span], jnp.concatenate(means, axis=1)], axis=0)
    logit[...] = jnp.dot(
        w_ref[...].reshape(NF * GP, 2 * FD), x, preferred_element_type=F32
    ).reshape(NF, GP, 2 * BLK)
    part_ref[:, :, span] = logit[...].astype(BF)
    mine_ref[:, span] = logit[feat]
    grads[...] += lax.dot_general(x, gl, NT, preferred_element_type=F32)

    @pl.when(step == NB // 2 - 1)
    def _():
        for b in range(NB):
            own_ref[:, b * BLK : (b + 1) * BLK] = acc[b]
        place = slot_place()
        for z in range(NZ):
            block = (acc[NB + z] * live[0:1, z * BLK : (z + 1) * BLK]).astype(BF)
            zero = jnp.zeros_like(block)
            wide = jnp.concatenate(
                [jnp.concatenate([block, zero], axis=1), jnp.concatenate([zero, block], axis=1)],
                axis=0,
            )
            back = lax.dot_general(place, wide, NT, preferred_element_type=F32)
            back_ref[:, z] = back.astype(BF).reshape(NX, CAP, BLK)

        @pl.loop(0, PARTS * HB)
        def _(h):
            hubg_ref[h] = acc[NB + NZ + h].astype(BF)

        total = grads[...] * float(PARTS * ROWS_DEV) ** (-0.5)
        for j in range(16):
            pair = jnp.concatenate([total[4 * j : 4 * j + 4], total[FD + 4 * j : FD + 4 * j + 4]], axis=0)
            for f in range(NF):
                pg_ref[f, j] = jnp.concatenate(
                    [pair[:, f * GP : (f + 1) * GP], jnp.zeros((8, BLK - GP), F32)], axis=1
                )


def layer(src, tiles, hidden, halo, hubs, counts, gl, w):
    outs = (
        jax.ShapeDtypeStruct((FD, ROWS_DEV), F32),
        jax.ShapeDtypeStruct((NX, NZ, CAP, BLK), BF),
        jax.ShapeDtypeStruct((PARTS * HB, FD, BLK), BF),
        jax.ShapeDtypeStruct((NF, GP, ROWS_DEV), BF),
        jax.ShapeDtypeStruct((GP, ROWS_DEV), F32),
        jax.ShapeDtypeStruct((NF, 16, 8, BLK), F32),
    )
    return pl.pallas_call(
        layer_kernel,
        grid=(NB // 2,),
        out_shape=outs,
        in_specs=[
            spec(pltpu.SMEM),
            pl.BlockSpec((2, TPB, BLK, BLK), lambda i: (i, 0, 0, 0)),
        ]
        + [spec()] * 6,
        out_specs=(spec(),) * 6,
        scratch_shapes=[
            VM((EXT, TR, BLK), BF),
            VM((16, PARTS * CAP), F32),
            VM((EXT, FD, BLK), F32),
            VM((2 * FD, NF * GP), BF),
            VM((NF, GP, 2 * BLK), F32),
            VM((2 * FD, NF * GP), F32),
        ],
        compiler_params=pltpu.CompilerParams(vmem_limit_bytes=56 << 20),
    )(src, tiles, hidden, halo, hubs, counts, gl, w)


def finish_kernel(hub_ref, own_ref, rows_ref, first_ref, second_ref, sum_ref, out_ref):
    core = lax.rem(lax.axis_index("dom"), NC)
    flat = []
    for k in range(NZ * NX // 4):
        a = first_ref[pl.ds(4 * k, 4)]
        b = second_ref[pl.ds(4 * k, 4)]
        turned = jnp.stack([a, b], axis=1).reshape(BLK, BLK).astype(F32).T
        flat.append(jnp.where(core == 0, turned[0:FD], turned[FD:]).astype(BF))
    back = jnp.concatenate(flat, axis=1)
    rows = rows_ref[...]

    @pl.loop(0, ROWS_DEV // CHUNK)
    def _(i):
        start = pl.multiple_of(i * CHUNK, CHUNK)
        hot = one_hot_rows(rows, start, CHUNK)
        got = lax.dot_general(back, hot, NT, preferred_element_type=F32)
        out_ref[:, pl.ds(start, CHUNK)] = own_ref[:, pl.ds(start, CHUNK)] + got

    for i in range(HB):
        start = pl.multiple_of(hub_ref[0, i] * BLK, BLK)
        out_ref[:, pl.ds(start, BLK)] += sum_ref[i]


def finish(hub_blocks, own, rows, first, second, hub_sum):
    return pl.pallas_call(
        finish_kernel,
        out_shape=jax.ShapeDtypeStruct((FD, ROWS_DEV), F32),
        in_specs=[spec(pltpu.SMEM)] + [spec()] * 5,
        out_specs=spec(),
        compiler_params=pltpu.CompilerParams(vmem_limit_bytes=32 << 20),
    )(hub_blocks, own, rows, first, second, hub_sum)


def local(
    hidden,
    tiles,
    tile_src,
    hub_blocks,
    halo_rows,
    halo_counts,
    weight_self,
    weight_neigh,
    grad_logits,
):
    rows = halo_rows.reshape(1, PARTS * CAP)
    gl, w, hubs, halo = gather_all(
        hub_blocks, hidden, rows, grad_logits, weight_self, weight_neigh
    )
    hubs = hubs.reshape(PARTS * HB, FD, BLK)
    own, back, hubg, part, mine, pg = layer(
        tile_src, tiles, hidden, halo, hubs, halo_counts, gl, w
    )
    parts = lax.all_to_all(part, "feat", 0, 0, tiled=True)
    feat = lax.axis_index("feat")
    others = jnp.arange(NF)[:, None, None] != feat
    logits = (mine + jnp.where(others, parts.astype(F32), 0.0).sum(axis=0))[:GR].astype(BF)
    hub_sum = lax.psum_scatter(hubg.astype(F32), "dom", scatter_dimension=0, tiled=True)
    pg = lax.psum_scatter(pg.reshape(PARTS, 8, BLK), "dom", scatter_dimension=0, tiled=True)[0]
    moves = [
        ((16 * g + j) * NF + f, (16 * f + j) * NF + g)
        for g in range(NF)
        for j in range(16)
        for f in range(NF)
    ]
    pg = lax.ppermute(pg, ("dom", "feat"), moves)
    grad_self, grad_neigh = pg[:4, :GR].T, pg[4:, :GR].T
    back = jnp.broadcast_to(back.transpose(1, 0, 2, 3)[:, :, None], (NZ, NX, NC, CAP, BLK))
    back = lax.all_to_all(back.reshape(PARTS, CAP, BLK), "dom", 0, 0, tiled=True)
    back = back.reshape(NZ * NX, NC, CAP, BLK)
    grad_hidden = finish(hub_blocks, own, rows, back[:, 0], back[:, 1], hub_sum)
    return logits, grad_self, grad_neigh, grad_hidden


def solution(mesh):
    placed = (
        P("feat", "dom"),
        P("dom", None, None, None),
        P("dom", None),
        P("dom", None),
        P("dom", None, None),
        P(),
        P("feat", None),
        P("feat", None),
        P("feat", "dom"),
    )
    return jax.shard_map(
        local,
        mesh=mesh,
        in_specs=placed,
        out_specs=(P("feat", "dom"), P("feat", "dom"), P("feat", "dom"), P("feat", "dom")),
        check_vma=False,
    )
```

```python
import jax
import jax.numpy as jnp
from jax import lax
from jax.experimental import pallas as pl
from jax.experimental.pallas import tpu as pltpu
from jax.sharding import PartitionSpec as P

BF = jnp.bfloat16
F32 = jnp.float32
BLK = 128
ROWS_DEV = 4096
TPB = 12
HB = 2
CAP = 16
NB = 32
NZ, NX, NC, NF = 8, 4, 2, 4
PARTS = NZ * NX * NC
GR = 43
GP = 48
FD = 64
EXT = 168
TR = 80
VM = pltpu.VMEM
CHUNK = 512
NT = (((1,), (1,)), ((), ()))
TN = (((0,), (0,)), ((), ()))


def spec(space=pltpu.VMEM):
    return pl.BlockSpec(memory_space=space)


def one_hot_rows(rows, start, size):
    node = lax.broadcasted_iota(jnp.int32, (size, PARTS * CAP), 0) + start
    return (node == rows).astype(F32).astype(BF)


def place():
    dom = lax.axis_index("dom")
    return dom // (NX * NC), lax.rem(dom // NC, NX), lax.rem(dom, NC), lax.axis_index("feat")


def device(z, x, c, f):
    return ((lax.rem(z, NZ) * NX + lax.rem(x, NX)) * NC + c, lax.rem(f, NF))


def remote(src, dst, send, recv, target):
    return pltpu.make_async_remote_copy(
        src_ref=src,
        dst_ref=dst,
        send_sem=send,
        recv_sem=recv,
        device_id=target,
        device_id_type=pl.DeviceIdType.MESH,
    )


def meet(targets):
    barrier = pltpu.get_barrier_semaphore()
    for target in targets:
        pl.semaphore_signal(
            barrier, inc=1, device_id=target, device_id_type=pl.DeviceIdType.MESH
        )
    return barrier


HALF = ROWS_DEV // 2


def gather_kernel(
    hub_ref,
    hidden_ref,
    rows_ref,
    gl_in,
    ws_ref,
    wn_ref,
    gl_ref,
    w_ref,
    hubs_ref,
    halo_ref,
    wsend,
    total,
    outgoing,
    sibling,
    merged,
    planes,
    y_send,
    y_recv,
    w_send,
    w_recv,
    hx_send,
    hx_recv,
    hz_send,
    hz_recv,
    hc_send,
    hc_recv,
    c_send,
    c_recv,
    z_send,
    z_recv,
    x_send,
    x_recv,
):
    z, x, c, f = place()
    pair = device(z, x, 1 - c, f)
    barrier = meet(
        [device(z, x, c, f + o) for o in range(1, NF)]
        + [device(z + o, x, c, f) for o in range(1, NZ)]
        + [device(z, x + o, c, f) for o in range(1, NX)]
        + [pair]
    )

    gl_ref[f, 32:GP, :] = jnp.zeros((GP - 32, ROWS_DEV), BF)
    gl_ref[f, 0:GR, :] = gl_in[...]
    for g in range(NF):
        wsend[g] = jnp.zeros((GP, 2 * FD), BF)
        cols = slice(g * FD, (g + 1) * FD)
        wsend[g, 0:GR] = jnp.concatenate([ws_ref[:, cols], wn_ref[:, cols]], axis=1)
    w_ref[f] = wsend[f]
    for i in range(HB):
        wanted = hub_ref[0, i]
        piece = hidden_ref[:, 0:BLK]
        for b in range(1, NB):
            piece = jnp.where(wanted == b, hidden_ref[:, b * BLK : (b + 1) * BLK], piece)
        hubs_ref[z, x, c, i] = piece
    pl.semaphore_wait(barrier, NF + NZ + NX - 2)

    def y_copy(way, k, origin, half):
        part = gl_ref.at[lax.rem(origin + NF, NF), :, pl.ds(half * HALF, HALF)]
        target = device(z, x, c, f + (1 if way == 0 else NF - 1))
        return remote(part, part, y_send.at[way, k], y_recv.at[way, k], target)

    y_first = [y_copy(0, 0, f, 0), y_copy(1, 0, f, 1), y_copy(0, 1, f, 1), y_copy(1, 1, f, 0)]
    for copy in y_first:
        copy.start()

    hx = [
        remote(
            hubs_ref.at[z, x, c],
            hubs_ref.at[z, x, c],
            hx_send.at[o - 1],
            hx_recv.at[o - 1],
            device(z, x + o, c, f),
        )
        for o in range(1, NX)
    ]
    for copy in hx:
        copy.start()
    ws = [
        remote(
            wsend.at[lax.rem(f + o, NF)],
            w_ref.at[f],
            w_send.at[o - 1],
            w_recv.at[o - 1],
            device(z, x, c, f + o),
        )
        for o in range(1, NF)
    ]
    for copy in ws:
        copy.start()

    def hz_copy(way, k, half):
        origin = lax.rem(z + (NZ - k if way == 0 else k), NZ)
        part = hubs_ref.at[origin, pl.ds(2 * half, 2), c]
        target = device(z + (1 if way == 0 else NZ - 1), x, c, f)
        return remote(part, part, hz_send.at[way, k, half], hz_recv.at[way, k, half], target)

    def hc_copy(k, half):
        part = hubs_ref.at[lax.rem(z + k, NZ), pl.ds(2 * half, 2), c]
        return remote(part, part, hc_send.at[k, half], hc_recv.at[k, half], pair)

    def hc_recv_wait(k, half):
        part = hubs_ref.at[lax.rem(z + k, NZ), pl.ds(2 * half, 2), 1 - c]
        remote(part, part, hc_send.at[k, half], hc_recv.at[k, half], pair).wait_recv()

    def hz_wait(way, k, half):
        origin = lax.rem(z + (NZ - k - 1 if way == 0 else k + 1), NZ)
        part = hubs_ref.at[origin, pl.ds(2 * half, 2), c]
        remote(part, part, hz_send.at[way, k, half], hz_recv.at[way, k, half], pair).wait_recv()

    sent = []

    def go(copy):
        copy.start()
        sent.append(copy)

    rows = rows_ref[...]
    total[...] = jnp.zeros_like(total)

    def gather(first, last):
        @pl.loop(first, last)
        def _(i):
            start = pl.multiple_of(i * CHUNK, CHUNK)
            hot = one_hot_rows(rows, start, CHUNK)
            total[...] += jnp.dot(
                hidden_ref[:, pl.ds(start, CHUNK)], hot, preferred_element_type=F32
            )

    gather(0, 3)
    for o in range(1, NX):
        part = hubs_ref.at[z, lax.rem(x + NX - o, NX), c]
        remote(part, part, hx_send.at[o - 1], hx_recv.at[o - 1], pair).wait_recv()
    for half in (0, 1):
        go(hz_copy(0, 0, half))
        go(hz_copy(1, 0, 1 - half))
    for half in (0, 1):
        go(hc_copy(0, half))
    gather(3, ROWS_DEV // CHUNK)
    for k in range(NZ):
        piece = total[:, k * BLK : (k + 1) * BLK]
        zero = jnp.zeros_like(piece)
        both = jnp.concatenate(
            [jnp.where(c == 0, piece, zero), jnp.where(c == 1, piece, zero)], axis=0
        )
        outgoing[k] = both.T.astype(BF).reshape(NX, NC, CAP, BLK)
    to_pair = remote(outgoing.at[:, :, 1 - c], sibling, c_send, c_recv, pair)
    go(to_pair)

    def y_wait(way, k, distance, half):
        origin = lax.rem(f + (NF - distance if way == 0 else distance), NF)
        part = gl_ref.at[origin, :, pl.ds(half * HALF, HALF)]
        remote(part, part, y_send.at[way, k], y_recv.at[way, k], pair).wait_recv()

    def ring(k):
        for half in (0, 1):
            for way in (0, 1):
                part = half if way == 0 else 1 - half
                if k == 3 and part != way:
                    continue
                hz_wait(way, k, part)
                if k < 2 or (k == 2 and part == way):
                    go(hz_copy(way, k + 1, part))
                go(hc_copy(NZ - k - 1 if way == 0 else k + 1, part))

    y_wait(0, 0, 1, 0)
    go(y_copy(0, 2, f - 1, 0))
    y_wait(1, 0, 1, 1)
    go(y_copy(1, 2, f + 1, 1))
    to_pair.wait_recv()
    merged[...] = outgoing[:, :, c] + sibling[...]
    for o in range(1, NZ):
        go(
            remote(
                merged.at[lax.rem(z + o, NZ)],
                planes.at[z],
                z_send.at[o - 1],
                z_recv.at[o - 1],
                device(z + o, x, c, f),
            )
        )
    planes[z] = merged[z]
    ring(0)
    for o in range(1, NZ):
        part = planes.at[lax.rem(z + NZ - o, NZ)]
        remote(part, part, z_send.at[o - 1], z_recv.at[o - 1], pair).wait_recv()
    for o in range(1, NX):
        go(
            remote(
                planes.at[:, lax.rem(x + o, NX)],
                halo_ref.at[x],
                x_send.at[o - 1],
                x_recv.at[o - 1],
                device(z, x + o, c, f),
            )
        )
    halo_ref[x] = planes[:, x]
    ring(1)
    for o in range(1, NX):
        part = halo_ref.at[lax.rem(x + NX - o, NX)]
        remote(part, part, x_send.at[o - 1], x_recv.at[o - 1], pair).wait_recv()
    ring(2)
    ring(3)
    for o in range(1, NF):
        part = w_ref.at[lax.rem(f + NF - o, NF)]
        remote(part, part, w_send.at[o - 1], w_recv.at[o - 1], pair).wait_recv()
    y_wait(0, 1, 1, 1)
    y_wait(1, 1, 1, 0)
    y_wait(0, 2, 2, 0)
    y_wait(1, 2, 2, 1)
    for k in range(NZ):
        for half in (0, 1):
            hc_recv_wait(k, half)
    for copy in y_first + hx + ws + sent:
        copy.wait_send()


def gather_all(hub_blocks, hidden, rows, grad_logits, weight_self, weight_neigh):
    dma = pltpu.SemaphoreType.DMA
    outs = (
        jax.ShapeDtypeStruct((NF, GP, ROWS_DEV), BF),
        jax.ShapeDtypeStruct((NF, GP, 2 * FD), BF),
        jax.ShapeDtypeStruct((NZ, NX, NC, HB, FD, BLK), BF),
        jax.ShapeDtypeStruct((NX, NZ, CAP, BLK), BF),
    )
    return pl.pallas_call(
        gather_kernel,
        out_shape=outs,
        in_specs=[spec(pltpu.SMEM)] + [spec()] * 5,
        out_specs=(spec(),) * 4,
        scratch_shapes=[
            VM((NF, GP, 2 * FD), BF),
            VM((FD, PARTS * CAP), F32),
            VM((NZ, NX, NC, CAP, BLK), BF),
            VM((NZ, NX, CAP, BLK), BF),
            VM((NZ, NX, CAP, BLK), BF),
            VM((NZ, NX, CAP, BLK), BF),
            dma((2, 3)),
            dma((2, 3)),
            dma((3,)),
            dma((3,)),
            dma((3,)),
            dma((3,)),
            dma((2, 4, 2)),
            dma((2, 4, 2)),
            dma((8, 2)),
            dma((8, 2)),
            dma,
            dma,
            dma((7,)),
            dma((7,)),
            dma((3,)),
            dma((3,)),
        ],
        compiler_params=pltpu.CompilerParams(
            collective_id=0, has_side_effects=True, vmem_limit_bytes=40 << 20
        ),
    )(hub_blocks, hidden, rows, grad_logits, weight_self, weight_neigh)


def slot_place():
    row = lax.broadcasted_iota(jnp.int32, (NX * CAP, NC * BLK), 0)
    lane = lax.broadcasted_iota(jnp.int32, (NX * CAP, NC * BLK), 1)
    want = (row // CAP) * (NC * CAP) + (lane // BLK) * CAP + row % CAP
    return (lane % BLK == want).astype(F32).astype(BF)


def layer_kernel(
    src_ref,
    tiles_ref,
    hidden_ref,
    halo_ref,
    hubs_ref,
    counts_ref,
    gl_ref,
    w_ref,
    own_ref,
    back_ref,
    hubg_ref,
    part_ref,
    mine_ref,
    pg_ref,
    table,
    live,
    acc,
    wt,
    logit,
    grads,
):
    step = pl.program_id(0)
    dom = lax.axis_index("dom")
    feat = lax.axis_index("feat")

    @pl.when(step == 0)
    def _():
        acc[...] = jnp.zeros_like(acc)
        grads[...] = jnp.zeros_like(grads)
        wt[...] = w_ref[...].reshape(NF * GP, 2 * FD).astype(F32).T.astype(BF)
        rows = TR - FD
        first = (lax.broadcasted_iota(jnp.int32, (rows, BLK), 0) == 0).astype(F32)
        ones = first.astype(BF)
        pick = (lax.broadcasted_iota(jnp.int32, (16, PARTS), 1) == dom).astype(F32).astype(BF)
        got = lax.dot_general(
            pick, counts_ref[...].astype(F32).astype(BF), NT, preferred_element_type=F32
        )
        sender = lax.broadcasted_iota(jnp.int32, (PARTS, PARTS * CAP), 0)
        column = lax.broadcasted_iota(jnp.int32, (PARTS, PARTS * CAP), 1)
        spread_out = (column // CAP == sender).astype(F32).astype(BF)
        limit = jnp.dot(got.astype(BF), spread_out, preferred_element_type=F32)
        slot = lax.broadcasted_iota(jnp.int32, (16, PARTS * CAP), 1) % CAP
        live[...] = (slot.astype(F32) < limit).astype(F32)
        for b in range(NB):
            table[b, 0:FD] = hidden_ref[:, b * BLK : (b + 1) * BLK]
            table[b, FD:TR] = ones
        place = slot_place()
        for z in range(NZ):
            rows_z = halo_ref[:, z].reshape(NX * CAP, BLK)
            res = lax.dot_general(rows_z, place, TN, preferred_element_type=F32)
            alive = live[0:1, z * BLK : (z + 1) * BLK]
            block = (res[0:FD, 0:BLK] + res[FD:, BLK:]) * alive
            table[NB + z, 0:FD] = block.astype(BF)
            table[NB + z, FD:TR] = (first * alive).astype(BF)

        @pl.loop(0, PARTS * HB)
        def _(h):
            table[NB + NZ + h, 0:FD] = hubs_ref[h]
            table[NB + NZ + h, FD:TR] = ones

    span = pl.ds(pl.multiple_of(step * (2 * BLK), 2 * BLK), 2 * BLK)
    gl = gl_ref[:, :, span].reshape(NF * GP, 2 * BLK)
    both = jnp.dot(wt[...], gl, preferred_element_type=F32)
    means = []
    for k in range(2):
        b = step * 2 + k
        picks = [src_ref[b, j] for j in range(TPB)]
        weights = jnp.concatenate([tiles_ref[k, j] for j in range(TPB)], axis=1)
        picked = jnp.concatenate([table[picks[j]] for j in range(TPB)], axis=1)
        summed = lax.dot_general(picked, weights, NT, preferred_element_type=F32)
        degree = summed[FD : FD + 1]
        means.append((summed[0:FD] / degree).astype(BF))
        lanes = slice(k * BLK, (k + 1) * BLK)
        scaled = (both[FD:, lanes] / degree).astype(BF)
        acc[b] += both[0:FD, lanes]
        pushed = jnp.dot(scaled, weights, preferred_element_type=F32)
        for j in range(TPB):
            acc[picks[j]] += pushed[:, j * BLK : (j + 1) * BLK]
    x = jnp.concatenate([hidden_ref[:, span], jnp.concatenate(means, axis=1)], axis=0)
    logit[...] = jnp.dot(
        w_ref[...].reshape(NF * GP, 2 * FD), x, preferred_element_type=F32
    ).reshape(NF, GP, 2 * BLK)
    part_ref[:, :, span] = logit[...].astype(BF)
    mine_ref[:, span] = logit[feat]
    grads[...] += lax.dot_general(x, gl, NT, preferred_element_type=F32)

    @pl.when(step == NB // 2 - 1)
    def _():
        for b in range(NB):
            own_ref[:, b * BLK : (b + 1) * BLK] = acc[b]
        place = slot_place()
        for z in range(NZ):
            block = (acc[NB + z] * live[0:1, z * BLK : (z + 1) * BLK]).astype(BF)
            zero = jnp.zeros_like(block)
            wide = jnp.concatenate(
                [jnp.concatenate([block, zero], axis=1), jnp.concatenate([zero, block], axis=1)],
                axis=0,
            )
            back = lax.dot_general(place, wide, NT, preferred_element_type=F32)
            back_ref[:, z] = back.astype(BF).reshape(NX, CAP, BLK)

        @pl.loop(0, PARTS * HB)
        def _(h):
            hubg_ref[h] = acc[NB + NZ + h].astype(BF)

        total = grads[...] * float(PARTS * ROWS_DEV) ** (-0.5)
        for j in range(16):
            pair = jnp.concatenate([total[4 * j : 4 * j + 4], total[FD + 4 * j : FD + 4 * j + 4]], axis=0)
            for f in range(NF):
                pg_ref[f, j] = jnp.concatenate(
                    [pair[:, f * GP : (f + 1) * GP], jnp.zeros((8, BLK - GP), F32)], axis=1
                )


def layer(src, tiles, hidden, halo, hubs, counts, gl, w):
    outs = (
        jax.ShapeDtypeStruct((FD, ROWS_DEV), F32),
        jax.ShapeDtypeStruct((NX, NZ, CAP, BLK), BF),
        jax.ShapeDtypeStruct((PARTS * HB, FD, BLK), BF),
        jax.ShapeDtypeStruct((NF, GP, ROWS_DEV), BF),
        jax.ShapeDtypeStruct((GP, ROWS_DEV), F32),
        jax.ShapeDtypeStruct((NF, 16, 8, BLK), F32),
    )
    return pl.pallas_call(
        layer_kernel,
        grid=(NB // 2,),
        out_shape=outs,
        in_specs=[
            spec(pltpu.SMEM),
            pl.BlockSpec((2, TPB, BLK, BLK), lambda i: (i, 0, 0, 0)),
        ]
        + [spec()] * 6,
        out_specs=(spec(),) * 6,
        scratch_shapes=[
            VM((EXT, TR, BLK), BF),
            VM((16, PARTS * CAP), F32),
            VM((EXT, FD, BLK), F32),
            VM((2 * FD, NF * GP), BF),
            VM((NF, GP, 2 * BLK), F32),
            VM((2 * FD, NF * GP), F32),
        ],
        compiler_params=pltpu.CompilerParams(vmem_limit_bytes=56 << 20),
    )(src, tiles, hidden, halo, hubs, counts, gl, w)


def return_kernel(
    hub_ref,
    rows_ref,
    own_ref,
    back_ref,
    hubg_ref,
    part_ref,
    mine_ref,
    pg_ref,
    logits_ref,
    gself_ref,
    gneigh_ref,
    out_ref,
    y_mid,
    y_stage,
    y_last,
    pairs,
    arrive,
    stage,
    x_stage,
    x_got,
    xsum,
    k_first,
    k_mine,
    k_pair,
    g_pair,
    g_sum,
    g_x,
    g_row,
    g_z,
    g_last,
    g_final,
    y_send,
    y_recv,
    pc_send,
    pc_recv,
    r_send,
    r_recv,
    rx_send,
    rx_recv,
    kx_send,
    kx_recv,
    kz_send,
    kz_recv,
    kc_send,
    kc_recv,
    gc_send,
    gc_recv,
    gx_send,
    gx_recv,
    gz_send,
    gz_recv,
    gm_send,
    gm_recv,
):
    z, x, c, f = place()
    pair = device(z, x, 1 - c, f)
    group = z // 2
    swap = device(2 * f + lax.rem(z, 2), x, c, group)
    barrier = meet(
        [device(z, x, c, f + o) for o in (1, NF - 1)]
        + [device(z + o, x, c, f) for o in range(1, NZ)]
        + [device(z, x + o, c, f) for o in range(1, NX)]
        + [pair]
    )

    @pl.when(f != group)
    def _():
        meet([swap])

    pl.semaphore_wait(barrier, jnp.where(f != group, 2 + NZ + NX, 1 + NZ + NX))
    sent = []

    def go(copy):
        copy.start()
        sent.append(copy)
        return copy

    def y_cols(half):
        return pl.ds(half * HALF, HALF)

    def y_copy(way, k, src, dst):
        target = device(z, x, c, f + (1 if way == 0 else NF - 1))
        return remote(src, dst, y_send.at[way, k], y_recv.at[way, k], target)

    def y_part(distance, half):
        return part_ref.at[lax.rem(f + distance, NF), :, y_cols(half)]

    y0 = [go(y_copy(w, 0, y_part(2, w), y_mid.at[w])) for w in (0, 1)]
    y1 = [
        go(y_copy(w, 1, y_part(1 if w == 0 else NF - 1, 1 - w), y_last.at[w, 1 - w]))
        for w in (0, 1)
    ]

    order = (4, 3, 5, 2, 6, 1, 7, 0)
    to_pair = {}
    for o in order:
        dest = lax.rem(z + o, NZ)
        to_pair[o] = go(
            remote(hubg_ref.at[dest, :, 1 - c], pairs.at[dest], pc_send.at[o], pc_recv.at[o], pair)
        )
    g_to_pair = go(remote(pg_ref.at[:, :, 1 - c], g_pair, gc_send, gc_recv, pair))
    kx = [
        go(
            remote(
                back_ref.at[lax.rem(x + o, NX)],
                k_first.at[x],
                kx_send.at[o - 1],
                kx_recv.at[o - 1],
                device(z, x + o, c, f),
            )
        )
        for o in range(1, NX)
    ]
    k_first[x] = back_ref[x]

    ring = {}

    def hub_step(k):
        distance = NZ // 2 - k
        for o in {distance, NZ - distance}:
            to_pair[o].wait_recv()
        for half in (0, 1):
            for way in (0, 1):
                h = half if way == 0 else 1 - half
                if k == 0 and h != way:
                    continue
                dest = lax.rem(z + (distance if way == 0 else NZ - distance), NZ)
                xs = slice(2 * h, 2 * h + 2)
                value = hubg_ref[dest, xs, c].astype(F32) + pairs[dest, xs].astype(F32)
                if k > 1 or (k == 1 and h == way):
                    ring[way, k - 1, h].wait_recv()
                    value = value + arrive[way, k - 1, h].astype(F32)
                stage[way, k, h] = value.astype(BF)
                ring[way, k, h] = go(
                    remote(
                        stage.at[way, k, h],
                        arrive.at[way, k, h],
                        r_send.at[way, k, h],
                        r_recv.at[way, k, h],
                        device(z + (1 if way == 0 else NZ - 1), x, c, f),
                    )
                )

    hub_step(0)
    for copy in kx:
        copy.wait_recv()
    kz = [
        go(
            remote(
                k_first.at[:, lax.rem(z + o, NZ)],
                k_mine.at[z],
                kz_send.at[o - 1],
                kz_recv.at[o - 1],
                device(z + o, x, c, f),
            )
        )
        for o in range(1, NZ)
    ]
    k_mine[z] = k_first[:, z]
    hub_step(1)

    y2 = []
    for w in (0, 1):
        y0[w].wait_recv()
        near = lax.rem(f + (1 if w == 0 else NF - 1), NF)
        value = part_ref[near, :, y_cols(w)].astype(F32) + y_mid[w].astype(F32)
        y_stage[w] = value.astype(BF)
        y2.append(go(y_copy(w, 2, y_stage.at[w], y_last.at[w, w])))

    for copy in kz:
        copy.wait_recv()
    kc = go(remote(k_mine, k_pair, kc_send, kc_recv, pair))
    hub_step(2)

    g_to_pair.wait_recv()
    g_sum[...] = pg_ref[:, :, c] + g_pair[...]
    gx = [
        go(
            remote(
                g_sum.at[:, lax.rem(x + o, NX)],
                g_x.at[o - 1],
                gx_send.at[o - 1],
                gx_recv.at[o - 1],
                device(z, x + o, c, f),
            )
        )
        for o in range(1, NX)
    ]

    kc.wait_recv()
    flat = []
    for k in range(NZ):
        a, b = k_mine[k], k_pair[k]
        first = jnp.where(c == 0, a, b)
        second = jnp.where(c == 0, b, a)
        turned = jnp.stack([first, second], axis=1).reshape(BLK, BLK).astype(F32).T
        flat.append(jnp.where(c == 0, turned[0:FD], turned[FD:]).astype(BF))
    back = jnp.concatenate(flat, axis=1)
    rows = rows_ref[...]

    def scatter(first, last):
        @pl.loop(first, last)
        def _(i):
            start = pl.multiple_of(i * CHUNK, CHUNK)
            hot = one_hot_rows(rows, start, CHUNK)
            got = lax.dot_general(back, hot, NT, preferred_element_type=F32)
            out_ref[:, pl.ds(start, CHUNK)] = own_ref[:, pl.ds(start, CHUNK)] + got

    scatter(0, 3)
    hub_step(3)
    for copy in gx:
        copy.wait_recv()
    g_row[...] = g_sum[:, x] + g_x[0] + g_x[1] + g_x[2]
    gz = [
        go(
            remote(
                g_row.at[lax.rem(z + o, NZ)],
                g_z.at[o - 1],
                gz_send.at[o - 1],
                gz_recv.at[o - 1],
                device(z + o, x, c, f),
            )
        )
        for o in range(1, NZ)
    ]
    scatter(3, ROWS_DEV // CHUNK)

    for copy in gz:
        copy.wait_recv()
    done = g_row[z]
    for o in range(1, NZ):
        done = done + g_z[o - 1]
    g_last[...] = done
    move = remote(g_last, g_final, gm_send, gm_recv, swap)

    @pl.when(f != group)
    def _():
        move.start()

    @pl.when(f == group)
    def _():
        g_final[...] = done

    for half in (0, 1):
        xs = slice(2 * half, 2 * half + 2)
        value = hubg_ref[z, xs, c].astype(F32)
        if half == 0:
            to_pair[0].wait_recv()
        value = value + pairs[z, xs].astype(F32)
        for way in (0, 1):
            ring[way, 3, half].wait_recv()
            value = value + arrive[way, 3, half].astype(F32)
        xsum[xs] = value
    x_stage[...] = xsum[...].astype(BF)
    hx = [
        go(
            remote(
                x_stage.at[lax.rem(x + o, NX)],
                x_got.at[o - 1],
                rx_send.at[o - 1],
                rx_recv.at[o - 1],
                device(z, x + o, c, f),
            )
        )
        for o in range(1, NX)
    ]

    for copy in y1 + y2:
        copy.wait_recv()
    for half in (0, 1):
        cols = y_cols(half)
        value = mine_ref[0:GR, cols]
        for w in (0, 1):
            value = value + y_last[w, half, 0:GR].astype(F32)
        logits_ref[:, cols] = value.astype(BF)

    for copy in hx:
        copy.wait_recv()
    total = xsum[x]
    for o in range(1, NX):
        total = total + x_got[o - 1].astype(F32)
    for b in range(NB):
        cols = slice(b * BLK, (b + 1) * BLK)
        value = out_ref[:, cols]
        for i in range(HB):
            value = jnp.where(hub_ref[0, i] == b, value + total[i], value)
        out_ref[:, cols] = value

    @pl.when(f != group)
    def _():
        move.wait()

    turned = jnp.concatenate([g_final[...], jnp.zeros((BLK - 8, BLK), F32)], axis=0).T
    gself_ref[...] = turned[0:GR, 0:4]
    gneigh_ref[...] = turned[0:GR, 4:8]
    for copy in sent:
        copy.wait_send()


def return_all(hub_blocks, rows, own, back, hubg, part, mine, pg):
    dma = pltpu.SemaphoreType.DMA
    outs = (
        jax.ShapeDtypeStruct((GR, ROWS_DEV), BF),
        jax.ShapeDtypeStruct((GR, 4), F32),
        jax.ShapeDtypeStruct((GR, 4), F32),
        jax.ShapeDtypeStruct((FD, ROWS_DEV), F32),
    )
    return pl.pallas_call(
        return_kernel,
        out_shape=outs,
        in_specs=[spec(pltpu.SMEM)] + [spec()] * 7,
        out_specs=(spec(),) * 4,
        scratch_shapes=[
            VM((2, GP, HALF), BF),
            VM((2, GP, HALF), BF),
            VM((2, 2, GP, HALF), BF),
            VM((NZ, NX, HB, FD, BLK), BF),
            VM((2, 4, 2, 2, HB, FD, BLK), BF),
            VM((2, 4, 2, 2, HB, FD, BLK), BF),
            VM((NX, HB, FD, BLK), BF),
            VM((NX - 1, HB, FD, BLK), BF),
            VM((NX, HB, FD, BLK), F32),
            VM((NX, NZ, CAP, BLK), BF),
            VM((NZ, NX, CAP, BLK), BF),
            VM((NZ, NX, CAP, BLK), BF),
            VM((NZ, NX, 8, BLK), F32),
            VM((NZ, NX, 8, BLK), F32),
            VM((NX - 1, NZ, 8, BLK), F32),
            VM((NZ, 8, BLK), F32),
            VM((NZ - 1, 8, BLK), F32),
            VM((8, BLK), F32),
            VM((8, BLK), F32),
            dma((2, 3)),
            dma((2, 3)),
            dma((8,)),
            dma((8,)),
            dma((2, 4, 2)),
            dma((2, 4, 2)),
            dma((3,)),
            dma((3,)),
            dma((3,)),
            dma((3,)),
            dma((7,)),
            dma((7,)),
            dma,
            dma,
            dma,
            dma,
            dma((3,)),
            dma((3,)),
            dma((7,)),
            dma((7,)),
            dma,
            dma,
        ],
        compiler_params=pltpu.CompilerParams(
            collective_id=1, has_side_effects=True, vmem_limit_bytes=48 << 20
        ),
    )(hub_blocks, rows, own, back, hubg, part, mine, pg)


def local(
    hidden,
    tiles,
    tile_src,
    hub_blocks,
    halo_rows,
    halo_counts,
    weight_self,
    weight_neigh,
    grad_logits,
):
    rows = halo_rows.reshape(1, PARTS * CAP)
    gl, w, hubs, halo = gather_all(
        hub_blocks, hidden, rows, grad_logits, weight_self, weight_neigh
    )
    hubs = hubs.reshape(PARTS * HB, FD, BLK)
    own, back, hubg, part, mine, pg = layer(
        tile_src, tiles, hidden, halo, hubs, halo_counts, gl, w
    )
    hubg = hubg.reshape(NZ, NX, NC, HB, FD, BLK)
    pg = pg.reshape(NZ, NX, NC, 8, BLK)
    return return_all(hub_blocks, rows, own, back, hubg, part, mine, pg)


def solution(mesh):
    placed = (
        P("feat", "dom"),
        P("dom", None, None, None),
        P("dom", None),
        P("dom", None),
        P("dom", None, None),
        P(),
        P("feat", None),
        P("feat", None),
        P("feat", "dom"),
    )
    return jax.shard_map(
        local,
        mesh=mesh,
        in_specs=placed,
        out_specs=(P("feat", "dom"), P("feat", "dom"), P("feat", "dom"), P("feat", "dom")),
        check_vma=False,
    )
```

```python
import jax
import jax.numpy as jnp
from jax import lax
from jax.experimental import pallas as pl
from jax.experimental.pallas import tpu as pltpu
from jax.sharding import PartitionSpec as P

BF = jnp.bfloat16
F32 = jnp.float32
BLK = 128
ROWS_DEV = 4096
TPB = 12
HB = 2
CAP = 16
NB = 32
NZ, NX, NC, NF = 8, 4, 2, 4
PARTS = NZ * NX * NC
GR = 43
GP = 48
FD = 64
EXT = 168
TR = 80
VM = pltpu.VMEM
CHUNK = 512
NT = (((1,), (1,)), ((), ()))
TN = (((0,), (0,)), ((), ()))


def spec(space=pltpu.VMEM):
    return pl.BlockSpec(memory_space=space)


def one_hot_rows(rows, start, size):
    node = lax.broadcasted_iota(jnp.int32, (size, PARTS * CAP), 0) + start
    return (node == rows).astype(F32).astype(BF)


def place():
    dom = lax.axis_index("dom")
    return dom // (NX * NC), lax.rem(dom // NC, NX), lax.rem(dom, NC), lax.axis_index("feat")


def device(z, x, c, f):
    return ((lax.rem(z, NZ) * NX + lax.rem(x, NX)) * NC + c, lax.rem(f, NF))


def remote(src, dst, send, recv, target):
    return pltpu.make_async_remote_copy(
        src_ref=src,
        dst_ref=dst,
        send_sem=send,
        recv_sem=recv,
        device_id=target,
        device_id_type=pl.DeviceIdType.MESH,
    )


def meet(targets):
    barrier = pltpu.get_barrier_semaphore()
    for target in targets:
        pl.semaphore_signal(
            barrier, inc=1, device_id=target, device_id_type=pl.DeviceIdType.MESH
        )
    return barrier


def slot_place():
    row = lax.broadcasted_iota(jnp.int32, (NX * CAP, NC * BLK), 0)
    lane = lax.broadcasted_iota(jnp.int32, (NX * CAP, NC * BLK), 1)
    want = (row // CAP) * (NC * CAP) + (lane // BLK) * CAP + row % CAP
    return (lane % BLK == want).astype(F32).astype(BF)


HALF = ROWS_DEV // 2
SLOTS = PARTS * CAP
TILES = NB * TPB
PAIRS = (TILES + EXT) // 2
POS = 640
SRC = 256
HUB0 = NB + NZ
WIDE = 2 * BLK
LOADS = 8
FACTOR = float(PARTS * ROWS_DEV) ** (-0.5)


def sort_tiles(col, row, idx):
    lane = lax.broadcasted_iota(jnp.int32, (TILES, SRC), 1)
    member = (col == lane).astype(F32)
    count = jnp.sum(member, axis=0, keepdims=True)
    pairs = jnp.floor((count + 1.0) * 0.5)
    before = lax.broadcasted_iota(jnp.int32, (SRC, SRC), 0) < lax.broadcasted_iota(
        jnp.int32, (SRC, SRC), 1
    )
    wide = jnp.broadcast_to(pairs, (16, SRC)).astype(BF)
    offset = jnp.dot(wide, before.astype(F32).astype(BF), preferred_element_type=F32)[0:1]
    mine = lax.broadcasted_iota(jnp.int32, (TILES, TILES), 0)
    other = lax.broadcasted_iota(jnp.int32, (TILES, TILES), 1)
    same = jnp.logical_and(col == row, other < mine).astype(F32)
    rank = jnp.sum(same, axis=1, keepdims=True)
    pos = 2.0 * jnp.sum(member * offset, axis=1, keepdims=True) + rank
    slot = lax.broadcasted_iota(jnp.int32, (TILES, POS), 1).astype(F32)
    tile = lax.broadcasted_iota(jnp.int32, (TILES, 1), 0)
    source = col.astype(F32)
    hit = (pos == slot).astype(F32)
    later = (pos + 2.0 == slot).astype(F32)

    def total(values):
        return jnp.sum(values, axis=0, keepdims=True)

    valid = total(hit)
    block = total(hit * (tile // TPB).astype(F32)) + float(NB) * (1.0 - valid)
    keep = (total(hit * source) == total(later * source)).astype(F32)
    idx[...] = jnp.zeros_like(idx)
    idx[0:1, :] = total(hit * tile.astype(F32)).astype(jnp.int32)
    idx[1:2, :] = block.astype(jnp.int32)
    idx[2:3, :] = keep.astype(jnp.int32)
    idx[3:4, 0:SRC] = jnp.maximum(offset + pairs - 1.0, 0.0).astype(jnp.int32)
    idx[4:5, 0:SRC] = (count > 0.0).astype(jnp.int32)
    idx[5:6, 0:TILES] = row


def entry(idx, row, at, most):
    return jnp.minimum(jnp.maximum(idx[row, at], 0), most)


def sage_kernel(
    hub_ref,
    tiles_hbm,
    hidden_ref,
    rows_ref,
    row_ref,
    col_ref,
    counts_ref,
    gl_in,
    ws_ref,
    wn_ref,
    logits_ref,
    gself_ref,
    gneigh_ref,
    out_ref,
    tiles,
    idx_v,
    idx,
    table,
    lives,
    live,
    gl_ref,
    wsend,
    w_ref,
    wt,
    total,
    outgoing,
    sibling,
    merged,
    planes,
    halo_ref,
    degree,
    scaled,
    runs,
    back_ref,
    hubg_ref,
    part_ref,
    mine_ref,
    logit,
    grads,
    pg_ref,
    y_mid,
    y_stage,
    y_last,
    pairs,
    arrive,
    stage,
    x_stage,
    x_got,
    xsum,
    k_first,
    k_mine,
    k_pair,
    g_pair,
    g_sum,
    g_x,
    g_row,
    g_z,
    g_last,
    g_final,
    t_sem,
    i_sem,
    gy_send,
    gy_recv,
    w_send,
    w_recv,
    hx_send,
    hx_recv,
    hz_send,
    hz_recv,
    hc_send,
    hc_recv,
    c_send,
    c_recv,
    z_send,
    z_recv,
    x_send,
    x_recv,
    y_send,
    y_recv,
    pc_send,
    pc_recv,
    r_send,
    r_recv,
    rx_send,
    rx_recv,
    kx_send,
    kx_recv,
    kz_send,
    kz_recv,
    kc_send,
    kc_recv,
    gc_send,
    gc_recv,
    gx_send,
    gx_recv,
    gz_send,
    gz_recv,
    gm_send,
    gm_recv,
):
    z, x, c, f = place()
    dom = lax.axis_index("dom")
    pair = device(z, x, 1 - c, f)
    group = z // 2
    swap = device(2 * f + lax.rem(z, 2), x, c, group)
    barrier = meet(
        [device(z, x, c, f + o) for o in range(1, NF)]
        + [device(z + o, x, c, f) for o in range(1, NZ)]
        + [device(z, x + o, c, f) for o in range(1, NX)]
        + [pair]
    )

    @pl.when(f != group)
    def _():
        meet([swap])

    loads = [
        pltpu.make_async_copy(
            tiles_hbm.at[pl.ds(i * (NB // LOADS), NB // LOADS)],
            tiles.at[pl.ds(i * (NB // LOADS), NB // LOADS)],
            t_sem.at[i],
        )
        for i in range(LOADS)
    ]
    for copy in loads:
        copy.start()
    sent = []

    def go(copy):
        copy.start()
        sent.append(copy)
        return copy

    gl_ref[f, 32:GP, :] = jnp.zeros((GP - 32, ROWS_DEV), BF)
    gl_ref[f, 0:GR, :] = gl_in[...]
    for g in range(NF):
        wsend[g] = jnp.zeros((GP, 2 * FD), BF)
        cols = slice(g * FD, (g + 1) * FD)
        wsend[g, 0:GR] = jnp.concatenate([ws_ref[:, cols], wn_ref[:, cols]], axis=1)
    w_ref[f] = wsend[f]

    def hub_at(core, plane, column, length):
        return pl.ds(HUB0 + core * 64 + plane * 8 + column * 2, length)

    for i in range(HB):
        wanted = hub_ref[0, i]
        piece = hidden_ref[:, 0:BLK]
        for b in range(1, NB):
            piece = jnp.where(wanted == b, hidden_ref[:, b * BLK : (b + 1) * BLK], piece)
        table[HUB0 + c * 64 + z * 8 + x * 2 + i] = piece
    for b in range(NB):
        table[b] = hidden_ref[:, b * BLK : (b + 1) * BLK]
    sort_tiles(col_ref[...], row_ref[...], idx_v)
    idx_copy = pltpu.make_async_copy(idx_v, idx, i_sem)
    idx_copy.start()

    pick = (lax.broadcasted_iota(jnp.int32, (16, PARTS), 1) == dom).astype(F32).astype(BF)
    got = lax.dot_general(
        pick, counts_ref[...].astype(F32).astype(BF), NT, preferred_element_type=F32
    )
    sender = lax.broadcasted_iota(jnp.int32, (PARTS, SLOTS), 0)
    column = lax.broadcasted_iota(jnp.int32, (PARTS, SLOTS), 1)
    spread_out = (column // CAP == sender).astype(F32).astype(BF)
    limit = jnp.dot(got.astype(BF), spread_out, preferred_element_type=F32)
    slot = lax.broadcasted_iota(jnp.int32, (16, SLOTS), 1) % CAP
    live[...] = (slot.astype(F32) < limit).astype(F32)
    lives[...] = jnp.ones_like(lives)
    for k in range(NZ):
        lives[NB + k] = live[:, k * BLK : (k + 1) * BLK].astype(BF)

    rows = rows_ref[...]
    total[...] = jnp.zeros_like(total)

    @pl.loop(0, ROWS_DEV // CHUNK)
    def _(i):
        start = pl.multiple_of(i * CHUNK, CHUNK)
        hot = one_hot_rows(rows, start, CHUNK)
        total[...] += jnp.dot(hidden_ref[:, pl.ds(start, CHUNK)], hot, preferred_element_type=F32)

    for k in range(NZ):
        piece = total[:, k * BLK : (k + 1) * BLK]
        zero = jnp.zeros_like(piece)
        both = jnp.concatenate(
            [jnp.where(c == 0, piece, zero), jnp.where(c == 1, piece, zero)], axis=0
        )
        outgoing[k] = both.T.astype(BF).reshape(NX, NC, CAP, BLK)
    idx_copy.wait()

    pl.semaphore_wait(barrier, jnp.where(f != group, NF + NZ + NX - 1, NF + NZ + NX - 2))

    def gy_copy(way, k, origin, half):
        part = gl_ref.at[lax.rem(origin + NF, NF), :, pl.ds(half * HALF, HALF)]
        target = device(z, x, c, f + (1 if way == 0 else NF - 1))
        return remote(part, part, gy_send.at[way, k], gy_recv.at[way, k], target)

    def gy_wait(way, k, distance, half):
        origin = lax.rem(f + (NF - distance if way == 0 else distance), NF)
        part = gl_ref.at[origin, :, pl.ds(half * HALF, HALF)]
        remote(part, part, gy_send.at[way, k], gy_recv.at[way, k], pair).wait_recv()

    for k in (0, 1):
        go(gy_copy(0, k, f, k))
        go(gy_copy(1, k, f, 1 - k))
    for o in range(1, NX):
        part = table.at[hub_at(c, z, x, HB)]
        go(remote(part, part, hx_send.at[o - 1], hx_recv.at[o - 1], device(z, x + o, c, f)))
    to_pair = go(remote(outgoing.at[:, :, 1 - c], sibling, c_send, c_recv, pair))
    for o in range(1, NF):
        go(
            remote(
                wsend.at[lax.rem(f + o, NF)],
                w_ref.at[f],
                w_send.at[o - 1],
                w_recv.at[o - 1],
                device(z, x, c, f + o),
            )
        )

    def hz_copy(way, k, half):
        origin = lax.rem(z + (NZ - k if way == 0 else k), NZ)
        part = table.at[hub_at(c, origin, 2 * half, 2 * HB)]
        target = device(z + (1 if way == 0 else NZ - 1), x, c, f)
        return remote(part, part, hz_send.at[way, k, half], hz_recv.at[way, k, half], target)

    def hz_wait(way, k, half):
        origin = lax.rem(z + (NZ - k - 1 if way == 0 else k + 1), NZ)
        part = table.at[hub_at(c, origin, 2 * half, 2 * HB)]
        remote(part, part, hz_send.at[way, k, half], hz_recv.at[way, k, half], pair).wait_recv()

    def hc_copy(k, half):
        part = table.at[hub_at(c, lax.rem(z + k, NZ), 2 * half, 2 * HB)]
        return remote(part, part, hc_send.at[k, half], hc_recv.at[k, half], pair)

    def hc_wait(k, half):
        part = table.at[hub_at(1 - c, lax.rem(z + k, NZ), 2 * half, 2 * HB)]
        remote(part, part, hc_send.at[k, half], hc_recv.at[k, half], pair).wait_recv()

    def ring(k):
        for half in (0, 1):
            for way in (0, 1):
                part = half if way == 0 else 1 - half
                if k == 3 and part != way:
                    continue
                hz_wait(way, k, part)
                if k < 2 or (k == 2 and part == way):
                    go(hz_copy(way, k + 1, part))
                go(hc_copy(NZ - k - 1 if way == 0 else k + 1, part))

    def block_weights(b):
        return jnp.concatenate([tiles[b, j] for j in range(TPB)], axis=1)

    def degrees(part):
        for i in range(part * LOADS // 4, (part + 1) * LOADS // 4):
            loads[i].wait()

        @pl.loop(part * (NB // 4), (part + 1) * (NB // 4))
        def _(b):
            alive = jnp.concatenate([lives[entry(idx, 5, b * TPB + j, EXT - 1)] for j in range(TPB)], axis=1)
            degree[b] = lax.dot_general(
                alive, block_weights(b), NT, preferred_element_type=F32
            )[0:8]

    degrees(0)
    for o in range(1, NX):
        part = table.at[hub_at(c, z, lax.rem(x + NX - o, NX), HB)]
        remote(part, part, hx_send.at[o - 1], hx_recv.at[o - 1], pair).wait_recv()
    for half in (0, 1):
        go(hz_copy(0, 0, half))
        go(hz_copy(1, 0, 1 - half))
    for half in (0, 1):
        go(hc_copy(0, half))
    to_pair.wait_recv()
    merged[...] = outgoing[:, :, c] + sibling[...]
    for o in range(1, NZ):
        go(
            remote(
                merged.at[lax.rem(z + o, NZ)],
                planes.at[z],
                z_send.at[o - 1],
                z_recv.at[o - 1],
                device(z + o, x, c, f),
            )
        )
    planes[z] = merged[z]
    degrees(1)
    gy_wait(0, 0, 1, 0)
    go(gy_copy(0, 2, f - 1, 0))
    gy_wait(1, 0, 1, 1)
    go(gy_copy(1, 2, f + 1, 1))
    ring(0)
    degrees(2)
    for o in range(1, NZ):
        part = planes.at[lax.rem(z + NZ - o, NZ)]
        remote(part, part, z_send.at[o - 1], z_recv.at[o - 1], pair).wait_recv()
    for o in range(1, NX):
        go(
            remote(
                planes.at[:, lax.rem(x + o, NX)],
                halo_ref.at[x],
                x_send.at[o - 1],
                x_recv.at[o - 1],
                device(z, x + o, c, f),
            )
        )
    halo_ref[x] = planes[:, x]
    ring(1)
    degrees(3)
    for o in range(1, NX):
        part = halo_ref.at[lax.rem(x + NX - o, NX)]
        remote(part, part, x_send.at[o - 1], x_recv.at[o - 1], pair).wait_recv()
    place_slots = slot_place()
    for k in range(NZ):
        res = lax.dot_general(
            halo_ref[:, k].reshape(NX * CAP, BLK), place_slots, TN, preferred_element_type=F32
        )
        alive = live[0:1, k * BLK : (k + 1) * BLK]
        table[NB + k] = ((res[0:FD, 0:BLK] + res[FD:, BLK:]) * alive).astype(BF)
    for o in range(1, NF):
        part = w_ref.at[lax.rem(f + NF - o, NF)]
        remote(part, part, w_send.at[o - 1], w_recv.at[o - 1], pair).wait_recv()
    wt[...] = w_ref[...].reshape(NF * GP, 2 * FD).astype(F32).T.astype(BF)
    grads[...] = jnp.zeros_like(grads)
    scaled[NB] = jnp.zeros((FD, BLK), BF)
    ring(2)
    gy_wait(0, 1, 1, 1)
    gy_wait(1, 1, 1, 0)
    gy_wait(0, 2, 2, 0)
    gy_wait(1, 2, 2, 1)

    def columns(step):
        return pl.ds(pl.multiple_of(step * WIDE, WIDE), WIDE)

    @pl.loop(0, NB // 2)
    def _(step):
        gl = gl_ref[:, :, columns(step)].reshape(NF * GP, WIDE)
        both = jnp.dot(wt[...], gl, preferred_element_type=F32)
        out_ref[:, columns(step)] = both[0:FD]
        for k in range(2):
            b = step * 2 + k
            part = both[FD:, k * BLK : (k + 1) * BLK] / degree[b, 0:1]
            scaled[b] = part.astype(BF)

    def push(k, run):
        flat = tiles.reshape(TILES, BLK, BLK)
        spots = (2 * k, 2 * k + 1)
        left = jnp.concatenate([scaled[entry(idx, 1, q, NB)] for q in spots], axis=1)
        right = jnp.concatenate([flat[entry(idx, 0, q, TILES - 1)] for q in spots], axis=0)
        run = jnp.where(idx[2, 2 * k] == 1, run, 0.0)
        run = run + jnp.dot(left, right, preferred_element_type=F32)
        runs[k] = run
        return run

    lax.fori_loop(0, PAIRS, push, jnp.zeros((FD, BLK), F32), unroll=6)

    def returned(source):
        return jnp.where(idx[4, source] == 1, runs[entry(idx, 3, source, PAIRS - 1)], 0.0)

    @pl.loop(0, PARTS * HB)
    def _(h):
        hubg_ref[h] = returned(HUB0 + h).astype(BF)

    def hub_rows(core, plane):
        return pl.ds(core * 64 + plane * 8, 8)

    order = (4, 3, 5, 2, 6, 1, 7, 0)
    hub_pair = {}
    for o in order:
        dest = lax.rem(z + o, NZ)
        hub_pair[o] = go(
            remote(
                hubg_ref.at[hub_rows(1 - c, dest)],
                pairs.at[dest],
                pc_send.at[o],
                pc_recv.at[o],
                pair,
            )
        )
    for k in range(NZ):
        block = (returned(NB + k) * live[0:1, k * BLK : (k + 1) * BLK]).astype(BF)
        zero = jnp.zeros_like(block)
        wide = jnp.concatenate(
            [jnp.concatenate([block, zero], axis=1), jnp.concatenate([zero, block], axis=1)],
            axis=0,
        )
        back = lax.dot_general(place_slots, wide, NT, preferred_element_type=F32)
        back_ref[:, k] = back.astype(BF).reshape(NX, CAP, BLK)
    kx = [
        go(
            remote(
                back_ref.at[lax.rem(x + o, NX)],
                k_first.at[x],
                kx_send.at[o - 1],
                kx_recv.at[o - 1],
                device(z, x + o, c, f),
            )
        )
        for o in range(1, NX)
    ]
    k_first[x] = back_ref[x]

    hops = {}

    def hub_step(k):
        distance = NZ // 2 - k
        for o in (distance, NZ - distance):
            if k > 0 or o == distance:
                if (o, "got") not in hops:
                    hub_pair[o].wait_recv()
                    hops[o, "got"] = True
        for half in (0, 1):
            for way in (0, 1):
                h = half if way == 0 else 1 - half
                if k == 0 and h != way:
                    continue
                dest = lax.rem(z + (distance if way == 0 else NZ - distance), NZ)
                value = hubg_ref[pl.ds(c * 64 + dest * 8 + 4 * h, 4)].astype(F32)
                value = value + pairs[dest, 4 * h : 4 * h + 4].astype(F32)
                if k > 1 or (k == 1 and h == way):
                    hops[way, k - 1, h].wait_recv()
                    value = value + arrive[way, k - 1, h].astype(F32)
                stage[way, k, h] = value.astype(BF)
                hops[way, k, h] = go(
                    remote(
                        stage.at[way, k, h],
                        arrive.at[way, k, h],
                        r_send.at[way, k, h],
                        r_recv.at[way, k, h],
                        device(z + (1 if way == 0 else NZ - 1), x, c, f),
                    )
                )

    hub_step(0)
    ring(3)
    for k in range(NZ):
        for half in (0, 1):
            hc_wait(k, half)

    def forward(part):
        @pl.loop(part * (NB // 8), (part + 1) * (NB // 8))
        def _(step):
            gl = gl_ref[:, :, columns(step)].reshape(NF * GP, WIDE)
            means = []
            for k in range(2):
                b = step * 2 + k
                picked = jnp.concatenate(
                    [table[entry(idx, 5, b * TPB + j, EXT - 1)] for j in range(TPB)], axis=1
                )
                summed = lax.dot_general(
                    picked, block_weights(b), NT, preferred_element_type=F32
                )
                means.append((summed / degree[b, 0:1]).astype(BF))
            both = jnp.concatenate(
                [hidden_ref[:, columns(step)], jnp.concatenate(means, axis=1)], axis=0
            )
            logit[...] = jnp.dot(
                w_ref[...].reshape(NF * GP, 2 * FD), both, preferred_element_type=F32
            ).reshape(NF, GP, WIDE)
            part_ref[:, :, columns(step)] = logit[...].astype(BF)
            mine_ref[:, columns(step)] = logit[f]
            grads[...] += lax.dot_general(both, gl, NT, preferred_element_type=F32)

    def y_cols(half):
        return pl.ds(half * HALF, HALF)

    def y_copy(way, k, src, dst):
        target = device(z, x, c, f + (1 if way == 0 else NF - 1))
        return remote(src, dst, y_send.at[way, k], y_recv.at[way, k], target)

    def y_part(distance, half):
        return part_ref.at[lax.rem(f + distance, NF), :, y_cols(half)]

    y0, y1, y2 = {}, {}, {}

    def y_start(half):
        y0[half] = go(y_copy(half, 0, y_part(2, half), y_mid.at[half]))
        way = 1 - half
        y1[way] = go(
            y_copy(way, 1, y_part(1 if way == 0 else NF - 1, half), y_last.at[way, half])
        )

    def y_pass(w):
        y0[w].wait_recv()
        near = lax.rem(f + (1 if w == 0 else NF - 1), NF)
        value = part_ref[near, :, y_cols(w)].astype(F32) + y_mid[w].astype(F32)
        y_stage[w] = value.astype(BF)
        y2[w] = go(y_copy(w, 2, y_stage.at[w], y_last.at[w, w]))

    forward(0)
    for copy in kx:
        copy.wait_recv()
    kz = [
        go(
            remote(
                k_first.at[:, lax.rem(z + o, NZ)],
                k_mine.at[z],
                kz_send.at[o - 1],
                kz_recv.at[o - 1],
                device(z + o, x, c, f),
            )
        )
        for o in range(1, NZ)
    ]
    k_mine[z] = k_first[:, z]
    forward(1)
    y_start(0)
    hub_step(1)
    forward(2)
    forward(3)
    y_start(1)

    scores = grads[...] * FACTOR
    for j in range(16):
        rows_j = slice(4 * j, 4 * j + 4)
        far_j = slice(FD + 4 * j, FD + 4 * j + 4)
        both_j = jnp.concatenate([scores[rows_j], scores[far_j]], axis=0)
        for g in range(NF):
            pg_ref[2 * g + j // 8, j // 2 % 4, j % 2] = jnp.concatenate(
                [both_j[:, g * GP : (g + 1) * GP], jnp.zeros((8, BLK - GP), F32)], axis=1
            )
    g_to_pair = go(remote(pg_ref.at[:, :, 1 - c], g_pair, gc_send, gc_recv, pair))
    for copy in kz:
        copy.wait_recv()
    kc = go(remote(k_mine, k_pair, kc_send, kc_recv, pair))
    hub_step(2)
    y_pass(0)

    g_to_pair.wait_recv()
    g_sum[...] = pg_ref[:, :, c] + g_pair[...]
    gx = [
        go(
            remote(
                g_sum.at[:, lax.rem(x + o, NX)],
                g_x.at[o - 1],
                gx_send.at[o - 1],
                gx_recv.at[o - 1],
                device(z, x + o, c, f),
            )
        )
        for o in range(1, NX)
    ]

    kc.wait_recv()
    flat_back = []
    for k in range(NZ):
        a, b = k_mine[k], k_pair[k]
        first = jnp.where(c == 0, a, b)
        second = jnp.where(c == 0, b, a)
        turned = jnp.stack([first, second], axis=1).reshape(BLK, BLK).astype(F32).T
        flat_back.append(jnp.where(c == 0, turned[0:FD], turned[FD:]).astype(BF))
    back = jnp.concatenate(flat_back, axis=1)

    def scatter(first, last):
        @pl.loop(first, last)
        def _(i):
            start = pl.multiple_of(i * CHUNK, CHUNK)
            hot = one_hot_rows(rows, start, CHUNK)
            got = lax.dot_general(back, hot, NT, preferred_element_type=F32)
            own = [returned(i * (CHUNK // BLK) + k) for k in range(CHUNK // BLK)]
            out_ref[:, pl.ds(start, CHUNK)] += got + jnp.concatenate(own, axis=1)

    scatter(0, 2)
    hub_step(3)
    y_pass(1)
    for copy in gx:
        copy.wait_recv()
    g_row[...] = g_sum[:, x] + g_x[0] + g_x[1] + g_x[2]
    gz = [
        go(
            remote(
                g_row.at[lax.rem(z + o, NZ)],
                g_z.at[o - 1],
                gz_send.at[o - 1],
                gz_recv.at[o - 1],
                device(z + o, x, c, f),
            )
        )
        for o in range(1, NZ)
    ]
    scatter(2, ROWS_DEV // CHUNK)

    for copy in gz:
        copy.wait_recv()
    done = g_row[z]
    for o in range(1, NZ):
        done = done + g_z[o - 1]
    g_last[...] = done
    move = remote(g_last, g_final, gm_send, gm_recv, swap)

    @pl.when(f != group)
    def _():
        move.start()

    @pl.when(f == group)
    def _():
        g_final[...] = done

    hub_pair[0].wait_recv()
    for half in (0, 1):
        span = slice(4 * half, 4 * half + 4)
        value = hubg_ref[pl.ds(c * 64 + z * 8 + 4 * half, 4)].astype(F32)
        value = value + pairs[z, span].astype(F32)
        for way in (0, 1):
            hops[way, 3, half].wait_recv()
            value = value + arrive[way, 3, half].astype(F32)
        xsum[span] = value
    x_stage[...] = xsum[...].astype(BF)
    rx = [
        go(
            remote(
                x_stage.at[pl.ds(lax.rem(x + o, NX) * HB, HB)],
                x_got.at[o - 1],
                rx_send.at[o - 1],
                rx_recv.at[o - 1],
                device(z, x + o, c, f),
            )
        )
        for o in range(1, NX)
    ]

    for w in (0, 1):
        y1[w].wait_recv()
        y2[w].wait_recv()
    for half in (0, 1):
        cols = y_cols(half)
        value = mine_ref[0:GR, cols]
        for w in (0, 1):
            value = value + y_last[w, half, 0:GR].astype(F32)
        logits_ref[:, cols] = value.astype(BF)

    for copy in rx:
        copy.wait_recv()
    summed = xsum[pl.ds(x * HB, HB)]
    for o in range(1, NX):
        summed = summed + x_got[o - 1].astype(F32)
    for b in range(NB):
        cols = slice(b * BLK, (b + 1) * BLK)
        value = out_ref[:, cols]
        for i in range(HB):
            value = jnp.where(hub_ref[0, i] == b, value + summed[i], value)
        out_ref[:, cols] = value

    @pl.when(f != group)
    def _():
        move.wait()

    turned = jnp.concatenate([g_final[...], jnp.zeros((BLK - 8, BLK), F32)], axis=0).T
    gself_ref[...] = turned[0:GR, 0:4]
    gneigh_ref[...] = turned[0:GR, 4:8]
    for copy in sent:
        copy.wait_send()


def sage(hub_blocks, tiles, hidden, rows, src_row, src_col, counts, gl, w_self, w_neigh):
    dma = pltpu.SemaphoreType.DMA
    outs = (
        jax.ShapeDtypeStruct((GR, ROWS_DEV), BF),
        jax.ShapeDtypeStruct((GR, 4), F32),
        jax.ShapeDtypeStruct((GR, 4), F32),
        jax.ShapeDtypeStruct((FD, ROWS_DEV), F32),
    )

    def both(*shape):
        return [dma(shape), dma(shape)]

    return pl.pallas_call(
        sage_kernel,
        out_shape=outs,
        in_specs=[spec(pltpu.SMEM), spec(pl.ANY)] + [spec()] * 8,
        out_specs=(spec(),) * 4,
        scratch_shapes=[
            VM((NB, TPB, BLK, BLK), BF),
            VM((8, POS), jnp.int32),
            pltpu.SMEM((8, POS), jnp.int32),
            VM((EXT, FD, BLK), BF),
            VM((EXT, 16, BLK), BF),
            VM((16, SLOTS), F32),
            VM((NF, GP, ROWS_DEV), BF),
            VM((NF, GP, 2 * FD), BF),
            VM((NF, GP, 2 * FD), BF),
            VM((2 * FD, NF * GP), BF),
            VM((FD, SLOTS), F32),
            VM((NZ, NX, NC, CAP, BLK), BF),
            VM((NZ, NX, CAP, BLK), BF),
            VM((NZ, NX, CAP, BLK), BF),
            VM((NZ, NX, CAP, BLK), BF),
            VM((NX, NZ, CAP, BLK), BF),
            VM((NB, 8, BLK), F32),
            VM((NB + 1, FD, BLK), BF),
            VM((PAIRS, FD, BLK), F32),
            VM((NX, NZ, CAP, BLK), BF),
            VM((PARTS * HB, FD, BLK), BF),
            VM((NF, GP, ROWS_DEV), BF),
            VM((GP, ROWS_DEV), F32),
            VM((NF, GP, WIDE), F32),
            VM((2 * FD, NF * GP), F32),
            VM((NZ, NX, NC, 8, BLK), F32),
            VM((2, GP, HALF), BF),
            VM((2, GP, HALF), BF),
            VM((2, 2, GP, HALF), BF),
            VM((NZ, 8, FD, BLK), BF),
            VM((2, 4, 2, 4, FD, BLK), BF),
            VM((2, 4, 2, 4, FD, BLK), BF),
            VM((8, FD, BLK), BF),
            VM((NX - 1, HB, FD, BLK), BF),
            VM((8, FD, BLK), F32),
            VM((NX, NZ, CAP, BLK), BF),
            VM((NZ, NX, CAP, BLK), BF),
            VM((NZ, NX, CAP, BLK), BF),
            VM((NZ, NX, 8, BLK), F32),
            VM((NZ, NX, 8, BLK), F32),
            VM((NX - 1, NZ, 8, BLK), F32),
            VM((NZ, 8, BLK), F32),
            VM((NZ - 1, 8, BLK), F32),
            VM((8, BLK), F32),
            VM((8, BLK), F32),
            dma((LOADS,)),
            dma,
        ]
        + both(2, 3)
        + both(3)
        + both(3)
        + both(2, 4, 2)
        + both(8, 2)
        + [dma, dma]
        + both(7)
        + both(3)
        + both(2, 3)
        + both(8)
        + both(2, 4, 2)
        + both(3)
        + both(3)
        + both(7)
        + [dma, dma]
        + [dma, dma]
        + both(3)
        + both(7)
        + [dma, dma],
        compiler_params=pltpu.CompilerParams(
            collective_id=0, has_side_effects=True, vmem_limit_bytes=60 << 20
        ),
    )(hub_blocks, tiles, hidden, rows, src_row, src_col, counts, gl, w_self, w_neigh)


def local(
    hidden,
    tiles,
    tile_src,
    hub_blocks,
    halo_rows,
    halo_counts,
    weight_self,
    weight_neigh,
    grad_logits,
):
    rows = halo_rows.reshape(1, PARTS * CAP)
    hub = tile_src - HUB0
    moved = HUB0 + hub // 2 % 2 * 64 + hub // 16 * 8 + hub // 4 % 4 * 2 + hub % 2
    src = jnp.where(tile_src < HUB0, tile_src, moved)
    return sage(
        hub_blocks,
        tiles,
        hidden,
        rows,
        src.reshape(1, TILES),
        src.reshape(TILES, 1),
        halo_counts,
        grad_logits,
        weight_self,
        weight_neigh,
    )


def solution(mesh):
    placed = (
        P("feat", "dom"),
        P("dom", None, None, None),
        P("dom", None),
        P("dom", None),
        P("dom", None, None),
        P(),
        P("feat", None),
        P("feat", None),
        P("feat", "dom"),
    )
    return jax.shard_map(
        local,
        mesh=mesh,
        in_specs=placed,
        out_specs=(P("feat", "dom"), P("feat", "dom"), P("feat", "dom"), P("feat", "dom")),
        check_vma=False,
    )
```

```python
import jax
import jax.numpy as jnp
from jax import lax
from jax.experimental import pallas as pl
from jax.experimental.pallas import tpu as pltpu
from jax.sharding import PartitionSpec as P

BF = jnp.bfloat16
F32 = jnp.float32
BLK = 128
ROWS_DEV = 4096
TPB = 12
HB = 2
CAP = 16
NB = 32
NZ, NX, NC, NF = 8, 4, 2, 4
PARTS = NZ * NX * NC
GR = 43
GP = 48
FD = 64
EXT = 168
TR = 80
VM = pltpu.VMEM
CHUNK = 512
NT = (((1,), (1,)), ((), ()))
TN = (((0,), (0,)), ((), ()))


def spec(space=pltpu.VMEM):
    return pl.BlockSpec(memory_space=space)


def one_hot_rows(rows, start, size):
    node = lax.broadcasted_iota(jnp.int32, (size, PARTS * CAP), 0) + start
    return (node == rows).astype(F32).astype(BF)


def place():
    dom = lax.axis_index("dom")
    return dom // (NX * NC), lax.rem(dom // NC, NX), lax.rem(dom, NC), lax.axis_index("feat")


def device(z, x, c, f):
    return ((lax.rem(z, NZ) * NX + lax.rem(x, NX)) * NC + c, lax.rem(f, NF))


def remote(src, dst, send, recv, target):
    return pltpu.make_async_remote_copy(
        src_ref=src,
        dst_ref=dst,
        send_sem=send,
        recv_sem=recv,
        device_id=target,
        device_id_type=pl.DeviceIdType.MESH,
    )


def meet(targets):
    barrier = pltpu.get_barrier_semaphore()
    for target in targets:
        pl.semaphore_signal(
            barrier, inc=1, device_id=target, device_id_type=pl.DeviceIdType.MESH
        )
    return barrier


def slot_place():
    row = lax.broadcasted_iota(jnp.int32, (NX * CAP, NC * BLK), 0)
    lane = lax.broadcasted_iota(jnp.int32, (NX * CAP, NC * BLK), 1)
    want = (row // CAP) * (NC * CAP) + (lane // BLK) * CAP + row % CAP
    return (lane % BLK == want).astype(F32).astype(BF)


HALF = ROWS_DEV // 2
SLOTS = PARTS * CAP
TILES = NB * TPB
PAIRS = (TILES + EXT) // 2
POS = 640
SRC = 256
HUB0 = NB + NZ
WIDE = 2 * BLK
LOADS = 8
FACTOR = float(PARTS * ROWS_DEV) ** (-0.5)


def sort_tiles(col, row, idx):
    lane = lax.broadcasted_iota(jnp.int32, (TILES, SRC), 1)
    member = (col == lane).astype(F32)
    count = jnp.sum(member, axis=0, keepdims=True)
    pairs = jnp.floor((count + 1.0) * 0.5)
    before = lax.broadcasted_iota(jnp.int32, (SRC, SRC), 0) < lax.broadcasted_iota(
        jnp.int32, (SRC, SRC), 1
    )
    wide = jnp.broadcast_to(pairs, (16, SRC)).astype(BF)
    offset = jnp.dot(wide, before.astype(F32).astype(BF), preferred_element_type=F32)[0:1]
    mine = lax.broadcasted_iota(jnp.int32, (TILES, TILES), 0)
    other = lax.broadcasted_iota(jnp.int32, (TILES, TILES), 1)
    same = jnp.logical_and(col == row, other < mine).astype(F32)
    rank = jnp.sum(same, axis=1, keepdims=True)
    pos = 2.0 * jnp.sum(member * offset, axis=1, keepdims=True) + rank
    slot = lax.broadcasted_iota(jnp.int32, (TILES, POS), 1).astype(F32)
    tile = lax.broadcasted_iota(jnp.int32, (TILES, 1), 0)
    source = col.astype(F32)
    hit = (pos == slot).astype(F32)
    later = (pos + 2.0 == slot).astype(F32)

    def total(values):
        return jnp.sum(values, axis=0, keepdims=True)

    valid = total(hit)
    block = total(hit * (tile // TPB).astype(F32)) + float(NB) * (1.0 - valid)
    keep = (total(hit * source) == total(later * source)).astype(F32)
    idx[...] = jnp.zeros_like(idx)
    idx[0:1, :] = total(hit * tile.astype(F32)).astype(jnp.int32)
    idx[1:2, :] = block.astype(jnp.int32)
    idx[2:3, :] = keep.astype(jnp.int32)
    idx[3:4, 0:SRC] = jnp.maximum(offset + pairs - 1.0, 0.0).astype(jnp.int32)
    idx[4:5, 0:SRC] = (count > 0.0).astype(jnp.int32)
    idx[5:6, 0:TILES] = row


def entry(idx, row, at, most):
    return jnp.minimum(jnp.maximum(idx[row, at], 0), most)


def sage_kernel(
    hub_ref,
    tiles_hbm,
    hidden_ref,
    halo_rows_ref,
    src_ref,
    counts_ref,
    gl_in,
    ws_ref,
    wn_ref,
    logits_ref,
    score_ref,
    sum_ref,
    out_ref,
    tiles,
    idx_v,
    idx,
    table,
    lives,
    live,
    gl_ref,
    wsend,
    w_ref,
    wt,
    total,
    outgoing,
    sibling,
    merged,
    planes,
    halo_ref,
    degree,
    scaled,
    runs,
    back_ref,
    hubg_ref,
    part_ref,
    mine_ref,
    logit,
    grads,
    pg_ref,
    y_mid,
    y_stage,
    y_last,
    pairs,
    arrive,
    stage,
    x_stage,
    x_got,
    xsum,
    b_stage,
    b_got,
    bsum,
    bz_stage,
    bz_got,
    k_first,
    k_mine,
    k_pair,
    g_pair,
    g_sum,
    g_x,
    g_row,
    g_z,
    g_last,
    g_final,
    t_sem,
    i_sem,
    gy_send,
    gy_recv,
    w_send,
    w_recv,
    hx_send,
    hx_recv,
    hz_send,
    hz_recv,
    hc_send,
    hc_recv,
    c_send,
    c_recv,
    z_send,
    z_recv,
    x_send,
    x_recv,
    y_send,
    y_recv,
    pc_send,
    pc_recv,
    r_send,
    r_recv,
    rx_send,
    rx_recv,
    bx_send,
    bx_recv,
    bz_send,
    bz_recv,
    kx_send,
    kx_recv,
    kz_send,
    kz_recv,
    kc_send,
    kc_recv,
    gc_send,
    gc_recv,
    gx_send,
    gx_recv,
    gz_send,
    gz_recv,
    gm_send,
    gm_recv,
):
    z, x, c, f = place()
    dom = lax.axis_index("dom")
    pair = device(z, x, 1 - c, f)
    group = z // 2
    swap = device(2 * f + lax.rem(z, 2), x, c, group)
    barrier = meet(
        [device(z, x, c, f + o) for o in range(1, NF)]
        + [device(z + o, x, c, f) for o in range(1, NZ)]
        + [device(z, x + o, c, f) for o in range(1, NX)]
        + [pair]
    )

    @pl.when(f != group)
    def _():
        meet([swap])

    loads = [
        pltpu.make_async_copy(
            tiles_hbm.at[pl.ds(i * (NB // LOADS), NB // LOADS)],
            tiles.at[pl.ds(i * (NB // LOADS), NB // LOADS)],
            t_sem.at[i],
        )
        for i in range(LOADS)
    ]
    for copy in loads:
        copy.start()
    sent = []

    def go(copy):
        copy.start()
        sent.append(copy)
        return copy

    gl_ref[f, 32:GP, :] = jnp.zeros((GP - 32, ROWS_DEV), BF)
    gl_ref[f, 0:GR, :] = gl_in[...]
    for g in range(NF):
        wsend[g] = jnp.zeros((GP, 2 * FD), BF)
        cols = slice(g * FD, (g + 1) * FD)
        wsend[g, 0:GR] = jnp.concatenate([ws_ref[:, cols], wn_ref[:, cols]], axis=1)
    w_ref[f] = wsend[f]

    def hub_at(core, plane, column, length):
        return pl.ds(HUB0 + core * 64 + plane * 8 + column * 2, length)

    for i in range(HB):
        wanted = hub_ref[0, i]
        piece = hidden_ref[:, 0:BLK]
        for b in range(1, NB):
            piece = jnp.where(wanted == b, hidden_ref[:, b * BLK : (b + 1) * BLK], piece)
        table[HUB0 + c * 64 + z * 8 + x * 2 + i] = piece
    for b in range(NB):
        table[b] = hidden_ref[:, b * BLK : (b + 1) * BLK]
    source = src_ref[...]
    hub = jnp.maximum(source - HUB0, 0)
    moved = HUB0 + (hub // 2 % 2) * 64 + (hub // 16) * 8 + (hub // 4 % 4) * 2 + hub % 2
    source = jnp.where(source < HUB0, source, moved).astype(F32).astype(BF)
    tile_lane = lax.broadcasted_iota(jnp.int32, (NB, TILES), 1)
    of_block = lax.broadcasted_iota(jnp.int32, (NB, TILES), 0) == tile_lane // TPB
    row = jnp.dot(source, of_block.astype(F32).astype(BF), preferred_element_type=F32)
    at = lax.broadcasted_iota(jnp.int32, (TPB, TILES), 1) % TPB
    row = jnp.where(at == lax.broadcasted_iota(jnp.int32, (TPB, TILES), 0), row, 0.0)
    row = jnp.sum(row, axis=0, keepdims=True).astype(jnp.int32)
    tile_row = lax.broadcasted_iota(jnp.int32, (TILES, NB), 0)
    of_block = lax.broadcasted_iota(jnp.int32, (TILES, NB), 1) == tile_row // TPB
    col = lax.dot_general(
        of_block.astype(F32).astype(BF), source, NT, preferred_element_type=F32
    )
    at = lax.broadcasted_iota(jnp.int32, (TILES, TPB), 0) % TPB
    col = jnp.where(at == lax.broadcasted_iota(jnp.int32, (TILES, TPB), 1), col, 0.0)
    col = jnp.sum(col, axis=1, keepdims=True).astype(jnp.int32)
    sort_tiles(col, row, idx_v)
    idx_copy = pltpu.make_async_copy(idx_v, idx, i_sem)
    idx_copy.start()

    pick = (lax.broadcasted_iota(jnp.int32, (16, PARTS), 1) == dom).astype(F32).astype(BF)
    got = lax.dot_general(
        pick, counts_ref[...].astype(F32).astype(BF), NT, preferred_element_type=F32
    )
    sender = lax.broadcasted_iota(jnp.int32, (PARTS, SLOTS), 0)
    column = lax.broadcasted_iota(jnp.int32, (PARTS, SLOTS), 1)
    spread_out = (column // CAP == sender).astype(F32).astype(BF)
    limit = jnp.dot(got.astype(BF), spread_out, preferred_element_type=F32)
    slot = lax.broadcasted_iota(jnp.int32, (16, SLOTS), 1) % CAP
    live[...] = (slot.astype(F32) < limit).astype(F32)
    lives[...] = jnp.ones_like(lives)
    for k in range(NZ):
        lives[NB + k] = live[:, k * BLK : (k + 1) * BLK].astype(BF)

    high = halo_rows_ref[...] // FD
    low = halo_rows_ref[...] - high * FD
    rows = sum(
        scale
        * jnp.dot(part.astype(F32).astype(BF), spread_out, preferred_element_type=F32)
        for part, scale in ((high, float(FD)), (low, 1.0))
    )
    at = lax.broadcasted_iota(jnp.int32, (CAP, SLOTS), 0)
    rows = jnp.sum(jnp.where(slot == at, rows, 0.0), axis=0, keepdims=True).astype(jnp.int32)
    total[...] = jnp.zeros_like(total)

    @pl.loop(0, ROWS_DEV // CHUNK)
    def _(i):
        start = pl.multiple_of(i * CHUNK, CHUNK)
        hot = one_hot_rows(rows, start, CHUNK)
        total[...] += jnp.dot(hidden_ref[:, pl.ds(start, CHUNK)], hot, preferred_element_type=F32)

    for k in range(NZ):
        piece = total[:, k * BLK : (k + 1) * BLK]
        zero = jnp.zeros_like(piece)
        both = jnp.concatenate(
            [jnp.where(c == 0, piece, zero), jnp.where(c == 1, piece, zero)], axis=0
        )
        outgoing[k] = both.T.astype(BF).reshape(NX, NC, CAP, BLK)
    idx_copy.wait()

    pl.semaphore_wait(barrier, jnp.where(f != group, NF + NZ + NX - 1, NF + NZ + NX - 2))

    def gy_copy(way, k, origin, half):
        part = gl_ref.at[lax.rem(origin + NF, NF), :, pl.ds(half * HALF, HALF)]
        target = device(z, x, c, f + (1 if way == 0 else NF - 1))
        return remote(part, part, gy_send.at[way, k], gy_recv.at[way, k], target)

    def gy_wait(way, k, distance, half):
        origin = lax.rem(f + (NF - distance if way == 0 else distance), NF)
        part = gl_ref.at[origin, :, pl.ds(half * HALF, HALF)]
        remote(part, part, gy_send.at[way, k], gy_recv.at[way, k], pair).wait_recv()

    for k in (0, 1):
        go(gy_copy(0, k, f, k))
        go(gy_copy(1, k, f, 1 - k))
    for o in range(1, NX):
        part = table.at[hub_at(c, z, x, HB)]
        go(remote(part, part, hx_send.at[o - 1], hx_recv.at[o - 1], device(z, x + o, c, f)))
    to_pair = go(remote(outgoing.at[:, :, 1 - c], sibling, c_send, c_recv, pair))
    for o in range(1, NF):
        go(
            remote(
                wsend.at[lax.rem(f + o, NF)],
                w_ref.at[f],
                w_send.at[o - 1],
                w_recv.at[o - 1],
                device(z, x, c, f + o),
            )
        )

    def hz_copy(way, k, half):
        origin = lax.rem(z + (NZ - k if way == 0 else k), NZ)
        part = table.at[hub_at(c, origin, 2 * half, 2 * HB)]
        target = device(z + (1 if way == 0 else NZ - 1), x, c, f)
        return remote(part, part, hz_send.at[way, k, half], hz_recv.at[way, k, half], target)

    def hz_wait(way, k, half):
        origin = lax.rem(z + (NZ - k - 1 if way == 0 else k + 1), NZ)
        part = table.at[hub_at(c, origin, 2 * half, 2 * HB)]
        remote(part, part, hz_send.at[way, k, half], hz_recv.at[way, k, half], pair).wait_recv()

    def hc_copy(k, half):
        part = table.at[hub_at(c, lax.rem(z + k, NZ), 2 * half, 2 * HB)]
        return remote(part, part, hc_send.at[k, half], hc_recv.at[k, half], pair)

    def hc_wait(k, half):
        part = table.at[hub_at(1 - c, lax.rem(z + k, NZ), 2 * half, 2 * HB)]
        remote(part, part, hc_send.at[k, half], hc_recv.at[k, half], pair).wait_recv()

    def ring(k):
        for half in (0, 1):
            for way in (0, 1):
                part = half if way == 0 else 1 - half
                if k == 3 and part != way:
                    continue
                hz_wait(way, k, part)
                if k < 2 or (k == 2 and part == way):
                    go(hz_copy(way, k + 1, part))
                go(hc_copy(NZ - k - 1 if way == 0 else k + 1, part))

    def block_weights(b):
        return jnp.concatenate([tiles[b, j] for j in range(TPB)], axis=1)

    def degrees(part):
        for i in range(part * LOADS // 4, (part + 1) * LOADS // 4):
            loads[i].wait()

        @pl.loop(part * (NB // 4), (part + 1) * (NB // 4))
        def _(b):
            alive = jnp.concatenate([lives[entry(idx, 5, b * TPB + j, EXT - 1)] for j in range(TPB)], axis=1)
            degree[b] = lax.dot_general(
                alive, block_weights(b), NT, preferred_element_type=F32
            )[0:8]

    degrees(0)
    for o in range(1, NX):
        part = table.at[hub_at(c, z, lax.rem(x + NX - o, NX), HB)]
        remote(part, part, hx_send.at[o - 1], hx_recv.at[o - 1], pair).wait_recv()
    for half in (0, 1):
        go(hz_copy(0, 0, half))
        go(hz_copy(1, 0, 1 - half))
    for half in (0, 1):
        go(hc_copy(0, half))
    to_pair.wait_recv()
    merged[...] = outgoing[:, :, c] + sibling[...]
    for o in range(1, NZ):
        go(
            remote(
                merged.at[lax.rem(z + o, NZ)],
                planes.at[z],
                z_send.at[o - 1],
                z_recv.at[o - 1],
                device(z + o, x, c, f),
            )
        )
    planes[z] = merged[z]
    degrees(1)
    gy_wait(0, 0, 1, 0)
    go(gy_copy(0, 2, f - 1, 0))
    gy_wait(1, 0, 1, 1)
    go(gy_copy(1, 2, f + 1, 1))
    ring(0)
    degrees(2)
    for o in range(1, NZ):
        part = planes.at[lax.rem(z + NZ - o, NZ)]
        remote(part, part, z_send.at[o - 1], z_recv.at[o - 1], pair).wait_recv()
    for o in range(1, NX):
        go(
            remote(
                planes.at[:, lax.rem(x + o, NX)],
                halo_ref.at[x],
                x_send.at[o - 1],
                x_recv.at[o - 1],
                device(z, x + o, c, f),
            )
        )
    halo_ref[x] = planes[:, x]
    ring(1)
    degrees(3)
    for o in range(1, NX):
        part = halo_ref.at[lax.rem(x + NX - o, NX)]
        remote(part, part, x_send.at[o - 1], x_recv.at[o - 1], pair).wait_recv()
    place_slots = slot_place()
    for k in range(NZ):
        res = lax.dot_general(
            halo_ref[:, k].reshape(NX * CAP, BLK), place_slots, TN, preferred_element_type=F32
        )
        alive = live[0:1, k * BLK : (k + 1) * BLK]
        table[NB + k] = ((res[0:FD, 0:BLK] + res[FD:, BLK:]) * alive).astype(BF)
    for o in range(1, NF):
        part = w_ref.at[lax.rem(f + NF - o, NF)]
        remote(part, part, w_send.at[o - 1], w_recv.at[o - 1], pair).wait_recv()
    wt[...] = w_ref[...].reshape(NF * GP, 2 * FD).astype(F32).T.astype(BF)
    grads[...] = jnp.zeros_like(grads)
    scaled[NB] = jnp.zeros((FD, BLK), BF)
    gy_wait(0, 1, 1, 1)
    gy_wait(1, 1, 1, 0)
    gy_wait(0, 2, 2, 0)
    gy_wait(1, 2, 2, 1)

    def columns(step):
        return pl.ds(pl.multiple_of(step * WIDE, WIDE), WIDE)

    @pl.loop(0, NB // 2)
    def _(step):
        gl = gl_ref[:, :, columns(step)].reshape(NF * GP, WIDE)
        both = jnp.dot(wt[...], gl, preferred_element_type=F32)
        out_ref[:, columns(step)] = both[0:FD]
        for k in range(2):
            b = step * 2 + k
            part = both[FD:, k * BLK : (k + 1) * BLK] / degree[b, 0:1]
            scaled[b] = part.astype(BF)

    ring(2)

    def push(k, run):
        flat = tiles.reshape(TILES, BLK, BLK)
        spots = (2 * k, 2 * k + 1)
        left = jnp.concatenate([scaled[entry(idx, 1, q, NB)] for q in spots], axis=1)
        right = jnp.concatenate([flat[entry(idx, 0, q, TILES - 1)] for q in spots], axis=0)
        run = jnp.where(idx[2, 2 * k] == 1, run, 0.0)
        run = run + jnp.dot(left, right, preferred_element_type=F32)
        runs[k] = run
        return run

    lax.fori_loop(0, PAIRS, push, jnp.zeros((FD, BLK), F32), unroll=23)

    def returned(source):
        return jnp.where(idx[4, source] == 1, runs[entry(idx, 3, source, PAIRS - 1)], 0.0)

    @pl.loop(0, PARTS * HB)
    def _(h):
        hubg_ref[h] = returned(HUB0 + h).astype(BF)

    def hub_rows(core, plane):
        return pl.ds(core * 64 + plane * 8, 8)

    order = (4, 3, 5, 2, 6, 1, 7, 0)
    hub_pair = {}
    for o in order:
        dest = lax.rem(z + o, NZ)
        hub_pair[o] = go(
            remote(
                hubg_ref.at[hub_rows(1 - c, dest)],
                pairs.at[dest],
                pc_send.at[o],
                pc_recv.at[o],
                pair,
            )
        )
    for k in range(NZ):
        block = (returned(NB + k) * live[0:1, k * BLK : (k + 1) * BLK]).astype(BF)
        zero = jnp.zeros_like(block)
        wide = jnp.concatenate(
            [jnp.concatenate([block, zero], axis=1), jnp.concatenate([zero, block], axis=1)],
            axis=0,
        )
        back = lax.dot_general(place_slots, wide, NT, preferred_element_type=F32)
        back_ref[:, k] = back.astype(BF).reshape(NX, CAP, BLK)
    kx = [
        go(
            remote(
                back_ref.at[lax.rem(x + o, NX)],
                k_first.at[x],
                kx_send.at[o - 1],
                kx_recv.at[o - 1],
                device(z, x + o, c, f),
            )
        )
        for o in range(1, NX)
    ]
    k_first[x] = back_ref[x]

    hops = {}
    seen = set()

    def from_pair(o):
        if o not in seen:
            seen.add(o)
            hub_pair[o].wait_recv()

    def hub_part(plane, first, length, half):
        low, high = half * FD // 2, (half + 1) * FD // 2
        mine = hubg_ref[pl.ds(c * 64 + plane * 8 + first, length), low:high]
        other = pairs[plane, pl.ds(first, length), low:high]
        return mine.astype(F32) + other.astype(F32)

    def hub_step(k):
        distance = NZ // 2 - k
        from_pair(distance)
        from_pair(NZ - distance)
        for half in (0, 1):
            for way in (0, 1):
                h = half if way == 0 else 1 - half
                if k == 0 and h != way:
                    continue
                dest = lax.rem(z + (distance if way == 0 else NZ - distance), NZ)
                value = hub_part(dest, 4 * h, 4, 0)
                if k > 1 or (k == 1 and h == way):
                    hops[way, k - 1, h].wait_recv()
                    value = value + arrive[way, k - 1, h].astype(F32)
                stage[way, k, h] = value.astype(BF)
                hops[way, k, h] = go(
                    remote(
                        stage.at[way, k, h],
                        arrive.at[way, k, h],
                        r_send.at[way, k, h],
                        r_recv.at[way, k, h],
                        device(z + (1 if way == 0 else NZ - 1), x, c, f),
                    )
                )

    hub_step(0)
    for o in range(NZ):
        from_pair(o)
    bx = []
    for o in range(1, NX):
        column_o = lax.rem(x + o, NX)

        @pl.loop(0, NZ)
        def _(plane):
            b_stage[o - 1, plane] = hub_part(plane, column_o * HB, HB, 1).astype(BF)

        bx.append(
            go(
                remote(
                    b_stage.at[o - 1],
                    b_got.at[o - 1],
                    bx_send.at[o - 1],
                    bx_recv.at[o - 1],
                    device(z, x + o, c, f),
                )
            )
        )
    ring(3)
    for k in range(NZ):
        for half in (0, 1):
            hc_wait(k, half)

    def forward(part):
        @pl.loop(part * (NB // 8), (part + 1) * (NB // 8))
        def _(step):
            gl = gl_ref[:, :, columns(step)].reshape(NF * GP, WIDE)
            means = []
            for k in range(2):
                b = step * 2 + k
                picked = jnp.concatenate(
                    [table[entry(idx, 5, b * TPB + j, EXT - 1)] for j in range(TPB)], axis=1
                )
                summed = lax.dot_general(
                    picked, block_weights(b), NT, preferred_element_type=F32
                )
                means.append((summed / degree[b, 0:1]).astype(BF))
            both = jnp.concatenate(
                [hidden_ref[:, columns(step)], jnp.concatenate(means, axis=1)], axis=0
            )
            logit[...] = jnp.dot(
                w_ref[...].reshape(NF * GP, 2 * FD), both, preferred_element_type=F32
            ).reshape(NF, GP, WIDE)
            part_ref[:, :, columns(step)] = logit[...].astype(BF)
            mine_ref[:, columns(step)] = logit[f]
            grads[...] += lax.dot_general(both, gl, NT, preferred_element_type=F32)

    def y_cols(half):
        return pl.ds(half * HALF, HALF)

    def y_copy(way, k, src, dst):
        target = device(z, x, c, f + (1 if way == 0 else NF - 1))
        return remote(src, dst, y_send.at[way, k], y_recv.at[way, k], target)

    def y_part(distance, half):
        return part_ref.at[lax.rem(f + distance, NF), :, y_cols(half)]

    y0, y1, y2 = {}, {}, {}

    def y_start(half):
        y0[half] = go(y_copy(half, 0, y_part(2, half), y_mid.at[half]))
        way = 1 - half
        y1[way] = go(
            y_copy(way, 1, y_part(1 if way == 0 else NF - 1, half), y_last.at[way, half])
        )

    def y_pass(w):
        y0[w].wait_recv()
        near = lax.rem(f + (1 if w == 0 else NF - 1), NF)
        value = part_ref[near, :, y_cols(w)].astype(F32) + y_mid[w].astype(F32)
        y_stage[w] = value.astype(BF)
        y2[w] = go(y_copy(w, 2, y_stage.at[w], y_last.at[w, w]))

    forward(0)
    for copy in kx:
        copy.wait_recv()
    kz = [
        go(
            remote(
                k_first.at[:, lax.rem(z + o, NZ)],
                k_mine.at[z],
                kz_send.at[o - 1],
                kz_recv.at[o - 1],
                device(z + o, x, c, f),
            )
        )
        for o in range(1, NZ)
    ]
    k_mine[z] = k_first[:, z]
    forward(1)
    y_start(0)
    hub_step(1)
    for copy in bx:
        copy.wait_recv()

    @pl.loop(0, NZ)
    def _(plane):
        value = hub_part(plane, x * HB, HB, 1)
        for o in range(1, NX):
            value = value + b_got[o - 1, plane].astype(F32)
        bsum[plane] = value
        bz_stage[plane] = value.astype(BF)

    bz = [
        go(
            remote(
                bz_stage.at[lax.rem(z + o, NZ)],
                bz_got.at[o - 1],
                bz_send.at[o - 1],
                bz_recv.at[o - 1],
                device(z + o, x, c, f),
            )
        )
        for o in range(1, NZ)
    ]
    forward(2)
    hub_step(2)
    forward(3)
    y_start(1)

    scores = grads[...] * FACTOR
    for j in range(16):
        rows_j = slice(4 * j, 4 * j + 4)
        far_j = slice(FD + 4 * j, FD + 4 * j + 4)
        both_j = jnp.concatenate([scores[rows_j], scores[far_j]], axis=0)
        for g in range(NF):
            pg_ref[2 * g + j // 8, j // 2 % 4, j % 2] = jnp.concatenate(
                [both_j[:, g * GP : (g + 1) * GP], jnp.zeros((8, BLK - GP), F32)], axis=1
            )
    g_to_pair = go(remote(pg_ref.at[:, :, 1 - c], g_pair, gc_send, gc_recv, pair))
    for copy in kz:
        copy.wait_recv()
    kc = go(remote(k_mine, k_pair, kc_send, kc_recv, pair))
    hub_step(3)
    y_pass(0)

    g_to_pair.wait_recv()
    g_sum[...] = pg_ref[:, :, c] + g_pair[...]
    gx = [
        go(
            remote(
                g_sum.at[:, lax.rem(x + o, NX)],
                g_x.at[o - 1],
                gx_send.at[o - 1],
                gx_recv.at[o - 1],
                device(z, x + o, c, f),
            )
        )
        for o in range(1, NX)
    ]

    kc.wait_recv()
    flat_back = []
    for k in range(NZ):
        a, b = k_mine[k], k_pair[k]
        first = jnp.where(c == 0, a, b)
        second = jnp.where(c == 0, b, a)
        turned = jnp.stack([first, second], axis=1).reshape(BLK, BLK).astype(F32).T
        flat_back.append(jnp.where(c == 0, turned[0:FD], turned[FD:]).astype(BF))
    back = jnp.concatenate(flat_back, axis=1)

    def scatter(first, last):
        @pl.loop(first, last)
        def _(i):
            start = pl.multiple_of(i * CHUNK, CHUNK)
            hot = one_hot_rows(rows, start, CHUNK)
            got = lax.dot_general(back, hot, NT, preferred_element_type=F32)
            own = [returned(i * (CHUNK // BLK) + k) for k in range(CHUNK // BLK)]
            out_ref[:, pl.ds(start, CHUNK)] += got + jnp.concatenate(own, axis=1)

    for half in (0, 1):
        value = hub_part(z, 4 * half, 4, 0)
        for way in (0, 1):
            hops[way, 3, half].wait_recv()
            value = value + arrive[way, 3, half].astype(F32)
        xsum[4 * half : 4 * half + 4] = value
    x_stage[...] = xsum[...].astype(BF)
    rx = [
        go(
            remote(
                x_stage.at[pl.ds(lax.rem(x + o, NX) * HB, HB)],
                x_got.at[o - 1],
                rx_send.at[o - 1],
                rx_recv.at[o - 1],
                device(z, x + o, c, f),
            )
        )
        for o in range(1, NX)
    ]
    y_pass(1)
    for copy in gx:
        copy.wait_recv()
    g_row[...] = g_sum[:, x] + g_x[0] + g_x[1] + g_x[2]
    gz = [
        go(
            remote(
                g_row.at[lax.rem(z + o, NZ)],
                g_z.at[o - 1],
                gz_send.at[o - 1],
                gz_recv.at[o - 1],
                device(z + o, x, c, f),
            )
        )
        for o in range(1, NZ)
    ]
    scatter(0, ROWS_DEV // CHUNK)

    for copy in gz:
        copy.wait_recv()
    done = g_row[z]
    for o in range(1, NZ):
        done = done + g_z[o - 1]
    g_last[...] = done
    move = remote(g_last, g_final, gm_send, gm_recv, swap)

    @pl.when(f != group)
    def _():
        move.start()

    @pl.when(f == group)
    def _():
        g_final[...] = done

    for copy in bz:
        copy.wait_recv()
    value = bsum[z]
    for o in range(1, NZ):
        value = value + bz_got[o - 1].astype(F32)
    sum_ref[:, FD // 2 :] = value
    for copy in rx:
        copy.wait_recv()
    value = xsum[pl.ds(x * HB, HB)]
    for o in range(1, NX):
        value = value + x_got[o - 1].astype(F32)
    sum_ref[:, 0 : FD // 2] = value

    for w in (0, 1):
        y1[w].wait_recv()
        y2[w].wait_recv()
    for half in (0, 1):
        cols = y_cols(half)
        value = mine_ref[0:GR, cols]
        for w in (0, 1):
            value = value + y_last[w, half, 0:GR].astype(F32)
        logits_ref[:, cols] = value.astype(BF)

    @pl.when(f != group)
    def _():
        move.wait()

    score_ref[...] = g_final[...]
    for copy in sent:
        copy.wait_send()


def sage(hub_blocks, tiles, hidden, rows, src, counts, gl, w_self, w_neigh):
    dma = pltpu.SemaphoreType.DMA
    outs = (
        jax.ShapeDtypeStruct((GR, ROWS_DEV), BF),
        jax.ShapeDtypeStruct((8, BLK), F32),
        jax.ShapeDtypeStruct((HB, FD, BLK), F32),
        jax.ShapeDtypeStruct((FD, ROWS_DEV), F32),
    )

    def both(*shape):
        return [dma(shape), dma(shape)]

    return pl.pallas_call(
        sage_kernel,
        out_shape=outs,
        in_specs=[spec(pltpu.SMEM), spec(pl.ANY)] + [spec()] * 7,
        out_specs=(spec(),) * 4,
        scratch_shapes=[
            VM((NB, TPB, BLK, BLK), BF),
            VM((8, POS), jnp.int32),
            pltpu.SMEM((8, POS), jnp.int32),
            VM((EXT, FD, BLK), BF),
            VM((EXT, 16, BLK), BF),
            VM((16, SLOTS), F32),
            VM((NF, GP, ROWS_DEV), BF),
            VM((NF, GP, 2 * FD), BF),
            VM((NF, GP, 2 * FD), BF),
            VM((2 * FD, NF * GP), BF),
            VM((FD, SLOTS), F32),
            VM((NZ, NX, NC, CAP, BLK), BF),
            VM((NZ, NX, CAP, BLK), BF),
            VM((NZ, NX, CAP, BLK), BF),
            VM((NZ, NX, CAP, BLK), BF),
            VM((NX, NZ, CAP, BLK), BF),
            VM((NB, 8, BLK), F32),
            VM((NB + 1, FD, BLK), BF),
            VM((PAIRS, FD, BLK), F32),
            VM((NX, NZ, CAP, BLK), BF),
            VM((PARTS * HB, FD, BLK), BF),
            VM((NF, GP, ROWS_DEV), BF),
            VM((GP, ROWS_DEV), F32),
            VM((NF, GP, WIDE), F32),
            VM((2 * FD, NF * GP), F32),
            VM((NZ, NX, NC, 8, BLK), F32),
            VM((2, GP, HALF), BF),
            VM((2, GP, HALF), BF),
            VM((2, 2, GP, HALF), BF),
            VM((NZ, 8, FD, BLK), BF),
            VM((2, 4, 2, 4, FD // 2, BLK), BF),
            VM((2, 4, 2, 4, FD // 2, BLK), BF),
            VM((8, FD // 2, BLK), BF),
            VM((NX - 1, HB, FD // 2, BLK), BF),
            VM((8, FD // 2, BLK), F32),
            VM((NX - 1, NZ, HB, FD // 2, BLK), BF),
            VM((NX - 1, NZ, HB, FD // 2, BLK), BF),
            VM((NZ, HB, FD // 2, BLK), F32),
            VM((NZ, HB, FD // 2, BLK), BF),
            VM((NZ - 1, HB, FD // 2, BLK), BF),
            VM((NX, NZ, CAP, BLK), BF),
            VM((NZ, NX, CAP, BLK), BF),
            VM((NZ, NX, CAP, BLK), BF),
            VM((NZ, NX, 8, BLK), F32),
            VM((NZ, NX, 8, BLK), F32),
            VM((NX - 1, NZ, 8, BLK), F32),
            VM((NZ, 8, BLK), F32),
            VM((NZ - 1, 8, BLK), F32),
            VM((8, BLK), F32),
            VM((8, BLK), F32),
            dma((LOADS,)),
            dma,
        ]
        + both(2, 3)
        + both(3)
        + both(3)
        + both(2, 4, 2)
        + both(8, 2)
        + [dma, dma]
        + both(7)
        + both(3)
        + both(2, 3)
        + both(8)
        + both(2, 4, 2)
        + both(3)
        + both(3)
        + both(7)
        + both(3)
        + both(7)
        + [dma, dma]
        + [dma, dma]
        + both(3)
        + both(7)
        + [dma, dma],
        compiler_params=pltpu.CompilerParams(
            collective_id=0, has_side_effects=True, vmem_limit_bytes=60 << 20
        ),
    )(hub_blocks, tiles, hidden, rows, src, counts, gl, w_self, w_neigh)


def finish_kernel(hub_ref, out_in, sum_in, logits_in, score_in, logits, gself, gneigh, out):
    out[...] = out_in[...]
    for i in range(HB):
        start = pl.multiple_of(hub_ref[0, i] * BLK, BLK)
        out[:, pl.ds(start, BLK)] += sum_in[i]
    logits[...] = logits_in[...]
    gself[...] = score_in[0:4, 0:GR]
    gneigh[...] = score_in[4:8, 0:GR]


def finish(hub_blocks, out, hub_sum, logits, score):
    outs = (
        jax.ShapeDtypeStruct((GR, ROWS_DEV), BF),
        jax.ShapeDtypeStruct((4, GR), F32),
        jax.ShapeDtypeStruct((4, GR), F32),
        jax.ShapeDtypeStruct((FD, ROWS_DEV), F32),
    )
    return pl.pallas_call(
        finish_kernel,
        out_shape=outs,
        in_specs=[spec(pltpu.SMEM)] + [spec()] * 4,
        out_specs=(spec(),) * 4,
        compiler_params=pltpu.CompilerParams(vmem_limit_bytes=60 << 20),
    )(hub_blocks, out, hub_sum, logits, score)


def local(
    hidden,
    tiles,
    tile_src,
    hub_blocks,
    halo_rows,
    halo_counts,
    weight_self,
    weight_neigh,
    grad_logits,
):
    logits, score, hub_sum, out = sage(
        hub_blocks,
        tiles,
        hidden,
        halo_rows[0].T,
        tile_src.T,
        halo_counts,
        grad_logits,
        weight_self,
        weight_neigh,
    )
    logits, gself, gneigh, out = finish(hub_blocks, out, hub_sum, logits, score)
    return logits, gself.T, gneigh.T, out


def solution(mesh):
    placed = (
        P("feat", "dom"),
        P("dom", None, None, None),
        P("dom", None),
        P("dom", None),
        P("dom", None, None),
        P(),
        P("feat", None),
        P("feat", None),
        P("feat", "dom"),
    )
    return jax.shard_map(
        local,
        mesh=mesh,
        in_specs=placed,
        out_specs=(P("feat", "dom"), P("feat", "dom"), P("feat", "dom"), P("feat", "dom")),
        check_vma=False,
    )
```

```python
import jax
import jax.numpy as jnp
from jax import lax
from jax.experimental import pallas as pl
from jax.experimental.pallas import tpu as pltpu
from jax.sharding import PartitionSpec as P

BF = jnp.bfloat16
F32 = jnp.float32
BLK = 128
ROWS_DEV = 4096
TPB = 12
HB = 2
CAP = 16
NB = 32
NZ, NX, NC, NF = 8, 4, 2, 4
PARTS = NZ * NX * NC
GR = 43
GP = 48
FD = 64
EXT = 168
TR = 80
VM = pltpu.VMEM
CHUNK = 512
NT = (((1,), (1,)), ((), ()))
TN = (((0,), (0,)), ((), ()))


def spec(space=pltpu.VMEM):
    return pl.BlockSpec(memory_space=space)


def one_hot_rows(rows, start, size):
    node = lax.broadcasted_iota(jnp.int32, (size, PARTS * CAP), 0) + start
    return (node == rows).astype(F32).astype(BF)


def place():
    dom = lax.axis_index("dom")
    return dom // (NX * NC), lax.rem(dom // NC, NX), lax.rem(dom, NC), lax.axis_index("feat")


def device(z, x, c, f):
    return ((lax.rem(z, NZ) * NX + lax.rem(x, NX)) * NC + c, lax.rem(f, NF))


def remote(src, dst, send, recv, target):
    return pltpu.make_async_remote_copy(
        src_ref=src,
        dst_ref=dst,
        send_sem=send,
        recv_sem=recv,
        device_id=target,
        device_id_type=pl.DeviceIdType.MESH,
    )


def meet(targets):
    barrier = pltpu.get_barrier_semaphore()
    for target in targets:
        pl.semaphore_signal(
            barrier, inc=1, device_id=target, device_id_type=pl.DeviceIdType.MESH
        )
    return barrier


def slot_place():
    row = lax.broadcasted_iota(jnp.int32, (NX * CAP, NC * BLK), 0)
    lane = lax.broadcasted_iota(jnp.int32, (NX * CAP, NC * BLK), 1)
    want = (row // CAP) * (NC * CAP) + (lane // BLK) * CAP + row % CAP
    return (lane % BLK == want).astype(F32).astype(BF)


HALF = ROWS_DEV // 2
SLOTS = PARTS * CAP
TILES = NB * TPB
PAIRS = (TILES + EXT) // 2
POS = 640
SRC = 256
HUB0 = NB + NZ
WIDE = 2 * BLK
LOADS = 8
FACTOR = float(PARTS * ROWS_DEV) ** (-0.5)


def sort_tiles(col, row, idx):
    lane = lax.broadcasted_iota(jnp.int32, (TILES, SRC), 1)
    member = (col == lane).astype(F32)
    count = jnp.sum(member, axis=0, keepdims=True)
    pairs = jnp.floor((count + 1.0) * 0.5)
    before = lax.broadcasted_iota(jnp.int32, (SRC, SRC), 0) < lax.broadcasted_iota(
        jnp.int32, (SRC, SRC), 1
    )
    wide = jnp.broadcast_to(pairs, (16, SRC)).astype(BF)
    offset = jnp.dot(wide, before.astype(F32).astype(BF), preferred_element_type=F32)[0:1]
    mine = lax.broadcasted_iota(jnp.int32, (TILES, TILES), 0)
    other = lax.broadcasted_iota(jnp.int32, (TILES, TILES), 1)
    same = jnp.logical_and(col == row, other < mine).astype(F32)
    rank = jnp.sum(same, axis=1, keepdims=True)
    pos = 2.0 * jnp.sum(member * offset, axis=1, keepdims=True) + rank
    slot = lax.broadcasted_iota(jnp.int32, (TILES, POS), 1).astype(F32)
    tile = lax.broadcasted_iota(jnp.int32, (TILES, 1), 0)
    source = col.astype(F32)
    hit = (pos == slot).astype(F32)
    later = (pos + 2.0 == slot).astype(F32)

    def total(values):
        return jnp.sum(values, axis=0, keepdims=True)

    valid = total(hit)
    block = total(hit * (tile // TPB).astype(F32)) + float(NB) * (1.0 - valid)
    keep = (total(hit * source) == total(later * source)).astype(F32)
    idx[...] = jnp.zeros_like(idx)
    idx[0:1, :] = total(hit * tile.astype(F32)).astype(jnp.int32)
    idx[1:2, :] = block.astype(jnp.int32)
    idx[2:3, :] = keep.astype(jnp.int32)
    idx[3:4, 0:SRC] = jnp.maximum(offset + pairs - 1.0, 0.0).astype(jnp.int32)
    idx[4:5, 0:SRC] = (count > 0.0).astype(jnp.int32)
    idx[5:6, 0:TILES] = row


def entry(idx, row, at, most):
    return jnp.minimum(jnp.maximum(idx[row, at], 0), most)


def sage_kernel(
    hub_ref,
    tiles_hbm,
    hidden_ref,
    halo_rows_ref,
    src_ref,
    counts_ref,
    gl_in,
    ws_ref,
    wn_ref,
    logits_ref,
    score_ref,
    sum_ref,
    out_ref,
    tiles,
    idx_v,
    idx,
    table,
    lives,
    live,
    gl_ref,
    wsend,
    w_ref,
    wt,
    total,
    outgoing,
    sibling,
    merged,
    planes,
    halo_ref,
    degree,
    scaled,
    runs,
    back_ref,
    hubg_ref,
    part_ref,
    mine_ref,
    logit,
    grads,
    pg_ref,
    y_mid,
    y_stage,
    y_last,
    pairs,
    arrive,
    stage,
    x_stage,
    x_got,
    xsum,
    b_stage,
    b_got,
    bsum,
    bz_stage,
    bz_got,
    k_first,
    k_mine,
    k_pair,
    g_pair,
    g_sum,
    g_x,
    g_row,
    g_z,
    g_last,
    g_final,
    t_sem,
    i_sem,
    gy_send,
    gy_recv,
    w_send,
    w_recv,
    hx_send,
    hx_recv,
    hz_send,
    hz_recv,
    hc_send,
    hc_recv,
    c_send,
    c_recv,
    z_send,
    z_recv,
    x_send,
    x_recv,
    y_send,
    y_recv,
    pc_send,
    pc_recv,
    r_send,
    r_recv,
    rx_send,
    rx_recv,
    bx_send,
    bx_recv,
    bz_send,
    bz_recv,
    kx_send,
    kx_recv,
    kz_send,
    kz_recv,
    kc_send,
    kc_recv,
    gc_send,
    gc_recv,
    gx_send,
    gx_recv,
    gz_send,
    gz_recv,
    gm_send,
    gm_recv,
):
    z, x, c, f = place()
    dom = lax.axis_index("dom")
    pair = device(z, x, 1 - c, f)
    group = z // 2
    swap = device(2 * f + lax.rem(z, 2), x, c, group)
    barrier = meet(
        [device(z, x, c, f + o) for o in range(1, NF)]
        + [device(z + o, x, c, f) for o in range(1, NZ)]
        + [device(z, x + o, c, f) for o in range(1, NX)]
        + [pair]
    )

    @pl.when(f != group)
    def _():
        meet([swap])

    loads = [
        pltpu.make_async_copy(
            tiles_hbm.at[pl.ds(i * (NB // LOADS), NB // LOADS)],
            tiles.at[pl.ds(i * (NB // LOADS), NB // LOADS)],
            t_sem.at[i],
        )
        for i in range(LOADS)
    ]
    for copy in loads:
        copy.start()
    sent = []

    def go(copy):
        copy.start()
        sent.append(copy)
        return copy

    gl_ref[f, 32:GP, :] = jnp.zeros((GP - 32, ROWS_DEV), BF)
    gl_ref[f, 0:GR, :] = gl_in[...]
    for g in range(NF):
        wsend[g] = jnp.zeros((GP, 2 * FD), BF)
        cols = slice(g * FD, (g + 1) * FD)
        wsend[g, 0:GR] = jnp.concatenate([ws_ref[:, cols], wn_ref[:, cols]], axis=1)
    w_ref[f] = wsend[f]

    def hub_at(core, plane, column, length):
        return pl.ds(HUB0 + core * 64 + plane * 8 + column * 2, length)

    for i in range(HB):
        wanted = hub_ref[0, i]
        piece = hidden_ref[:, 0:BLK]
        for b in range(1, NB):
            piece = jnp.where(wanted == b, hidden_ref[:, b * BLK : (b + 1) * BLK], piece)
        table[HUB0 + c * 64 + z * 8 + x * 2 + i] = piece
    for b in range(NB):
        table[b] = hidden_ref[:, b * BLK : (b + 1) * BLK]
    source = src_ref[...]
    hub = jnp.maximum(source - HUB0, 0)
    moved = HUB0 + (hub // 2 % 2) * 64 + (hub // 16) * 8 + (hub // 4 % 4) * 2 + hub % 2
    source = jnp.where(source < HUB0, source, moved).astype(F32).astype(BF)
    tile_lane = lax.broadcasted_iota(jnp.int32, (NB, TILES), 1)
    of_block = lax.broadcasted_iota(jnp.int32, (NB, TILES), 0) == tile_lane // TPB
    row = jnp.dot(source, of_block.astype(F32).astype(BF), preferred_element_type=F32)
    at = lax.broadcasted_iota(jnp.int32, (TPB, TILES), 1) % TPB
    row = jnp.where(at == lax.broadcasted_iota(jnp.int32, (TPB, TILES), 0), row, 0.0)
    row = jnp.sum(row, axis=0, keepdims=True).astype(jnp.int32)
    tile_row = lax.broadcasted_iota(jnp.int32, (TILES, NB), 0)
    of_block = lax.broadcasted_iota(jnp.int32, (TILES, NB), 1) == tile_row // TPB
    col = lax.dot_general(
        of_block.astype(F32).astype(BF), source, NT, preferred_element_type=F32
    )
    at = lax.broadcasted_iota(jnp.int32, (TILES, TPB), 0) % TPB
    col = jnp.where(at == lax.broadcasted_iota(jnp.int32, (TILES, TPB), 1), col, 0.0)
    col = jnp.sum(col, axis=1, keepdims=True).astype(jnp.int32)
    sort_tiles(col, row, idx_v)
    idx_copy = pltpu.make_async_copy(idx_v, idx, i_sem)
    idx_copy.start()

    pick = (lax.broadcasted_iota(jnp.int32, (16, PARTS), 1) == dom).astype(F32).astype(BF)
    got = lax.dot_general(
        pick, counts_ref[...].astype(F32).astype(BF), NT, preferred_element_type=F32
    )
    sender = lax.broadcasted_iota(jnp.int32, (PARTS, SLOTS), 0)
    column = lax.broadcasted_iota(jnp.int32, (PARTS, SLOTS), 1)
    spread_out = (column // CAP == sender).astype(F32).astype(BF)
    limit = jnp.dot(got.astype(BF), spread_out, preferred_element_type=F32)
    slot = lax.broadcasted_iota(jnp.int32, (16, SLOTS), 1) % CAP
    live[...] = (slot.astype(F32) < limit).astype(F32)
    lives[...] = jnp.ones_like(lives)
    for k in range(NZ):
        lives[NB + k] = live[:, k * BLK : (k + 1) * BLK].astype(BF)

    high = halo_rows_ref[...] // FD
    low = halo_rows_ref[...] - high * FD
    rows = sum(
        scale
        * jnp.dot(part.astype(F32).astype(BF), spread_out, preferred_element_type=F32)
        for part, scale in ((high, float(FD)), (low, 1.0))
    )
    at = lax.broadcasted_iota(jnp.int32, (CAP, SLOTS), 0)
    rows = jnp.sum(jnp.where(slot == at, rows, 0.0), axis=0, keepdims=True).astype(jnp.int32)
    total[...] = jnp.zeros_like(total)

    @pl.loop(0, ROWS_DEV // CHUNK)
    def _(i):
        start = pl.multiple_of(i * CHUNK, CHUNK)
        hot = one_hot_rows(rows, start, CHUNK)
        total[...] += jnp.dot(hidden_ref[:, pl.ds(start, CHUNK)], hot, preferred_element_type=F32)

    for k in range(NZ):
        piece = total[:, k * BLK : (k + 1) * BLK]
        zero = jnp.zeros_like(piece)
        both = jnp.concatenate(
            [jnp.where(c == 0, piece, zero), jnp.where(c == 1, piece, zero)], axis=0
        )
        outgoing[k] = both.T.astype(BF).reshape(NX, NC, CAP, BLK)
    idx_copy.wait()

    pl.semaphore_wait(barrier, jnp.where(f != group, NF + NZ + NX - 1, NF + NZ + NX - 2))

    def gy_copy(way, k, origin, half):
        part = gl_ref.at[lax.rem(origin + NF, NF), :, pl.ds(half * HALF, HALF)]
        target = device(z, x, c, f + (1 if way == 0 else NF - 1))
        return remote(part, part, gy_send.at[way, k], gy_recv.at[way, k], target)

    def gy_wait(way, k, distance, half):
        origin = lax.rem(f + (NF - distance if way == 0 else distance), NF)
        part = gl_ref.at[origin, :, pl.ds(half * HALF, HALF)]
        remote(part, part, gy_send.at[way, k], gy_recv.at[way, k], pair).wait_recv()

    for k in (0, 1):
        go(gy_copy(0, k, f, k))
        go(gy_copy(1, k, f, 1 - k))
    for o in range(1, NX):
        part = table.at[hub_at(c, z, x, HB)]
        go(remote(part, part, hx_send.at[o - 1], hx_recv.at[o - 1], device(z, x + o, c, f)))
    to_pair = go(remote(outgoing.at[:, :, 1 - c], sibling, c_send, c_recv, pair))
    for o in range(1, NF):
        go(
            remote(
                wsend.at[lax.rem(f + o, NF)],
                w_ref.at[f],
                w_send.at[o - 1],
                w_recv.at[o - 1],
                device(z, x, c, f + o),
            )
        )

    def hz_copy(way, k, half):
        origin = lax.rem(z + (NZ - k if way == 0 else k), NZ)
        part = table.at[hub_at(c, origin, 2 * half, 2 * HB)]
        target = device(z + (1 if way == 0 else NZ - 1), x, c, f)
        return remote(part, part, hz_send.at[way, k, half], hz_recv.at[way, k, half], target)

    def hz_wait(way, k, half):
        origin = lax.rem(z + (NZ - k - 1 if way == 0 else k + 1), NZ)
        part = table.at[hub_at(c, origin, 2 * half, 2 * HB)]
        remote(part, part, hz_send.at[way, k, half], hz_recv.at[way, k, half], pair).wait_recv()

    def hc_copy(k, half):
        part = table.at[hub_at(c, lax.rem(z + k, NZ), 2 * half, 2 * HB)]
        return remote(part, part, hc_send.at[k, half], hc_recv.at[k, half], pair)

    def hc_wait(k, half):
        part = table.at[hub_at(1 - c, lax.rem(z + k, NZ), 2 * half, 2 * HB)]
        remote(part, part, hc_send.at[k, half], hc_recv.at[k, half], pair).wait_recv()

    def ring(k):
        for half in (0, 1):
            for way in (0, 1):
                part = half if way == 0 else 1 - half
                if k == 3 and part != way:
                    continue
                hz_wait(way, k, part)
                if k < 2 or (k == 2 and part == way):
                    go(hz_copy(way, k + 1, part))
                go(hc_copy(NZ - k - 1 if way == 0 else k + 1, part))

    def block_weights(b):
        return jnp.concatenate([tiles[b, j] for j in range(TPB)], axis=1)

    def degrees(part):
        for i in range(part * LOADS // 4, (part + 1) * LOADS // 4):
            loads[i].wait()

        @pl.loop(part * (NB // 4), (part + 1) * (NB // 4))
        def _(b):
            alive = jnp.concatenate([lives[entry(idx, 5, b * TPB + j, EXT - 1)] for j in range(TPB)], axis=1)
            degree[b] = lax.dot_general(
                alive, block_weights(b), NT, preferred_element_type=F32
            )[0:8]

    degrees(0)
    for o in range(1, NX):
        part = table.at[hub_at(c, z, lax.rem(x + NX - o, NX), HB)]
        remote(part, part, hx_send.at[o - 1], hx_recv.at[o - 1], pair).wait_recv()
    for half in (0, 1):
        go(hz_copy(0, 0, half))
        go(hz_copy(1, 0, 1 - half))
    for half in (0, 1):
        go(hc_copy(0, half))
    to_pair.wait_recv()
    merged[...] = outgoing[:, :, c] + sibling[...]
    for o in range(1, NZ):
        go(
            remote(
                merged.at[lax.rem(z + o, NZ)],
                planes.at[z],
                z_send.at[o - 1],
                z_recv.at[o - 1],
                device(z + o, x, c, f),
            )
        )
    planes[z] = merged[z]
    degrees(1)
    gy_wait(0, 0, 1, 0)
    go(gy_copy(0, 2, f - 1, 0))
    gy_wait(1, 0, 1, 1)
    go(gy_copy(1, 2, f + 1, 1))
    ring(0)
    degrees(2)
    for o in range(1, NZ):
        part = planes.at[lax.rem(z + NZ - o, NZ)]
        remote(part, part, z_send.at[o - 1], z_recv.at[o - 1], pair).wait_recv()
    for o in range(1, NX):
        go(
            remote(
                planes.at[:, lax.rem(x + o, NX)],
                halo_ref.at[x],
                x_send.at[o - 1],
                x_recv.at[o - 1],
                device(z, x + o, c, f),
            )
        )
    halo_ref[x] = planes[:, x]
    ring(1)
    degrees(3)
    for o in range(1, NX):
        part = halo_ref.at[lax.rem(x + NX - o, NX)]
        remote(part, part, x_send.at[o - 1], x_recv.at[o - 1], pair).wait_recv()
    place_slots = slot_place()
    for k in range(NZ):
        res = lax.dot_general(
            halo_ref[:, k].reshape(NX * CAP, BLK), place_slots, TN, preferred_element_type=F32
        )
        alive = live[0:1, k * BLK : (k + 1) * BLK]
        table[NB + k] = ((res[0:FD, 0:BLK] + res[FD:, BLK:]) * alive).astype(BF)
    for o in range(1, NF):
        part = w_ref.at[lax.rem(f + NF - o, NF)]
        remote(part, part, w_send.at[o - 1], w_recv.at[o - 1], pair).wait_recv()
    wt[...] = w_ref[...].reshape(NF * GP, 2 * FD).astype(F32).T.astype(BF)
    grads[...] = jnp.zeros_like(grads)
    scaled[NB] = jnp.zeros((FD, BLK), BF)
    gy_wait(0, 1, 1, 1)
    gy_wait(1, 1, 1, 0)
    gy_wait(0, 2, 2, 0)
    gy_wait(1, 2, 2, 1)

    def columns(step):
        return pl.ds(pl.multiple_of(step * WIDE, WIDE), WIDE)

    @pl.loop(0, NB // 2, unroll=4)
    def _(step):
        gl = gl_ref[:, :, columns(step)].reshape(NF * GP, WIDE)
        both = jnp.dot(wt[...], gl, preferred_element_type=F32)
        out_ref[:, columns(step)] = both[0:FD]
        for k in range(2):
            b = step * 2 + k
            part = both[FD:, k * BLK : (k + 1) * BLK] / degree[b, 0:1]
            scaled[b] = part.astype(BF)

    ring(2)

    def push(k, run):
        flat = tiles.reshape(TILES, BLK, BLK)
        spots = (2 * k, 2 * k + 1)
        left = jnp.concatenate([scaled[entry(idx, 1, q, NB)] for q in spots], axis=1)
        right = jnp.concatenate([flat[entry(idx, 0, q, TILES - 1)] for q in spots], axis=0)
        run = jnp.where(idx[2, 2 * k] == 1, run, 0.0)
        run = run + jnp.dot(left, right, preferred_element_type=F32)
        runs[k] = run
        return run

    lax.fori_loop(0, PAIRS, push, jnp.zeros((FD, BLK), F32), unroll=23)

    def returned(source):
        return jnp.where(idx[4, source] == 1, runs[entry(idx, 3, source, PAIRS - 1)], 0.0)

    def collect(core):
        @pl.loop(0, PARTS * HB // NC, unroll=8)
        def _(h):
            at = core * (PARTS * HB // NC) + h
            hubg_ref[at] = returned(HUB0 + at).astype(BF)

    collect(1 - c)

    def hub_rows(core, plane):
        return pl.ds(core * 64 + plane * 8, 8)

    order = (4, 3, 5, 2, 6, 1, 7, 0)
    hub_pair = {}
    for o in order:
        dest = lax.rem(z + o, NZ)
        hub_pair[o] = go(
            remote(
                hubg_ref.at[hub_rows(1 - c, dest)],
                pairs.at[dest],
                pc_send.at[o],
                pc_recv.at[o],
                pair,
            )
        )
    collect(c)
    for k in range(NZ):
        block = (returned(NB + k) * live[0:1, k * BLK : (k + 1) * BLK]).astype(BF)
        zero = jnp.zeros_like(block)
        wide = jnp.concatenate(
            [jnp.concatenate([block, zero], axis=1), jnp.concatenate([zero, block], axis=1)],
            axis=0,
        )
        back = lax.dot_general(place_slots, wide, NT, preferred_element_type=F32)
        back_ref[:, k] = back.astype(BF).reshape(NX, CAP, BLK)
    kx = [
        go(
            remote(
                back_ref.at[lax.rem(x + o, NX)],
                k_first.at[x],
                kx_send.at[o - 1],
                kx_recv.at[o - 1],
                device(z, x + o, c, f),
            )
        )
        for o in range(1, NX)
    ]
    k_first[x] = back_ref[x]

    hops = {}
    seen = set()

    def from_pair(o):
        if o not in seen:
            seen.add(o)
            hub_pair[o].wait_recv()

    def hub_part(plane, first, length, half):
        low, high = half * FD // 2, (half + 1) * FD // 2
        mine = hubg_ref[pl.ds(c * 64 + plane * 8 + first, length), low:high]
        other = pairs[plane, pl.ds(first, length), low:high]
        return mine.astype(F32) + other.astype(F32)

    def hub_step(k):
        distance = NZ // 2 - k
        from_pair(distance)
        from_pair(NZ - distance)
        for half in (0, 1):
            for way in (0, 1):
                h = half if way == 0 else 1 - half
                if k == 0 and h != way:
                    continue
                dest = lax.rem(z + (distance if way == 0 else NZ - distance), NZ)
                value = hub_part(dest, 4 * h, 4, 0)
                if k > 1 or (k == 1 and h == way):
                    hops[way, k - 1, h].wait_recv()
                    value = value + arrive[way, k - 1, h].astype(F32)
                stage[way, k, h] = value.astype(BF)
                hops[way, k, h] = go(
                    remote(
                        stage.at[way, k, h],
                        arrive.at[way, k, h],
                        r_send.at[way, k, h],
                        r_recv.at[way, k, h],
                        device(z + (1 if way == 0 else NZ - 1), x, c, f),
                    )
                )

    hub_step(0)
    for o in range(NZ):
        from_pair(o)
    bx = []
    for o in range(1, NX):
        column_o = lax.rem(x + o, NX)

        @pl.loop(0, NZ, unroll=NZ)
        def _(plane):
            b_stage[o - 1, plane] = hub_part(plane, column_o * HB, HB, 1).astype(BF)

        bx.append(
            go(
                remote(
                    b_stage.at[o - 1],
                    b_got.at[o - 1],
                    bx_send.at[o - 1],
                    bx_recv.at[o - 1],
                    device(z, x + o, c, f),
                )
            )
        )
    ring(3)
    for k in range(NZ):
        for half in (0, 1):
            hc_wait(k, half)

    def forward(part):
        @pl.loop(part * (NB // 8), (part + 1) * (NB // 8), unroll=2)
        def _(step):
            gl = gl_ref[:, :, columns(step)].reshape(NF * GP, WIDE)
            means = []
            for k in range(2):
                b = step * 2 + k
                picked = jnp.concatenate(
                    [table[entry(idx, 5, b * TPB + j, EXT - 1)] for j in range(TPB)], axis=1
                )
                summed = lax.dot_general(
                    picked, block_weights(b), NT, preferred_element_type=F32
                )
                means.append((summed / degree[b, 0:1]).astype(BF))
            both = jnp.concatenate(
                [hidden_ref[:, columns(step)], jnp.concatenate(means, axis=1)], axis=0
            )
            logit[...] = jnp.dot(
                w_ref[...].reshape(NF * GP, 2 * FD), both, preferred_element_type=F32
            ).reshape(NF, GP, WIDE)
            part_ref[:, :, columns(step)] = logit[...].astype(BF)
            mine_ref[:, columns(step)] = logit[f]
            grads[...] += lax.dot_general(both, gl, NT, preferred_element_type=F32)

    def y_cols(half):
        return pl.ds(half * HALF, HALF)

    def y_copy(way, k, src, dst):
        target = device(z, x, c, f + (1 if way == 0 else NF - 1))
        return remote(src, dst, y_send.at[way, k], y_recv.at[way, k], target)

    def y_part(distance, half):
        return part_ref.at[lax.rem(f + distance, NF), :, y_cols(half)]

    y0, y1, y2 = {}, {}, {}

    def y_start(half):
        y0[half] = go(y_copy(half, 0, y_part(2, half), y_mid.at[half]))
        way = 1 - half
        y1[way] = go(
            y_copy(way, 1, y_part(1 if way == 0 else NF - 1, half), y_last.at[way, half])
        )

    def y_pass(w):
        y0[w].wait_recv()
        near = lax.rem(f + (1 if w == 0 else NF - 1), NF)
        value = part_ref[near, :, y_cols(w)].astype(F32) + y_mid[w].astype(F32)
        y_stage[w] = value.astype(BF)
        y2[w] = go(y_copy(w, 2, y_stage.at[w], y_last.at[w, w]))

    forward(0)
    for copy in kx:
        copy.wait_recv()
    kz = [
        go(
            remote(
                k_first.at[:, lax.rem(z + o, NZ)],
                k_mine.at[z],
                kz_send.at[o - 1],
                kz_recv.at[o - 1],
                device(z + o, x, c, f),
            )
        )
        for o in range(1, NZ)
    ]
    k_mine[z] = k_first[:, z]
    forward(1)
    y_start(0)
    hub_step(1)
    for copy in bx:
        copy.wait_recv()

    @pl.loop(0, NZ, unroll=NZ)
    def _(plane):
        value = hub_part(plane, x * HB, HB, 1)
        for o in range(1, NX):
            value = value + b_got[o - 1, plane].astype(F32)
        bsum[plane] = value
        bz_stage[plane] = value.astype(BF)

    bz = [
        go(
            remote(
                bz_stage.at[lax.rem(z + o, NZ)],
                bz_got.at[o - 1],
                bz_send.at[o - 1],
                bz_recv.at[o - 1],
                device(z + o, x, c, f),
            )
        )
        for o in range(1, NZ)
    ]
    forward(2)
    hub_step(2)
    forward(3)
    y_start(1)

    scores = grads[...] * FACTOR
    for j in range(16):
        rows_j = slice(4 * j, 4 * j + 4)
        far_j = slice(FD + 4 * j, FD + 4 * j + 4)
        both_j = jnp.concatenate([scores[rows_j], scores[far_j]], axis=0)
        for g in range(NF):
            pg_ref[2 * g + j // 8, j // 2 % 4, j % 2] = jnp.concatenate(
                [both_j[:, g * GP : (g + 1) * GP], jnp.zeros((8, BLK - GP), F32)], axis=1
            )
    g_to_pair = go(remote(pg_ref.at[:, :, 1 - c], g_pair, gc_send, gc_recv, pair))
    for copy in kz:
        copy.wait_recv()
    kc = go(remote(k_mine, k_pair, kc_send, kc_recv, pair))
    hub_step(3)
    y_pass(0)

    g_to_pair.wait_recv()
    g_sum[...] = pg_ref[:, :, c] + g_pair[...]
    gx = [
        go(
            remote(
                g_sum.at[:, lax.rem(x + o, NX)],
                g_x.at[o - 1],
                gx_send.at[o - 1],
                gx_recv.at[o - 1],
                device(z, x + o, c, f),
            )
        )
        for o in range(1, NX)
    ]

    kc.wait_recv()
    flat_back = []
    for k in range(NZ):
        a, b = k_mine[k], k_pair[k]
        first = jnp.where(c == 0, a, b)
        second = jnp.where(c == 0, b, a)
        turned = jnp.stack([first, second], axis=1).reshape(BLK, BLK).astype(F32).T
        flat_back.append(jnp.where(c == 0, turned[0:FD], turned[FD:]).astype(BF))
    back = jnp.concatenate(flat_back, axis=1)

    def scatter(first, last):
        @pl.loop(first, last)
        def _(i):
            start = pl.multiple_of(i * CHUNK, CHUNK)
            hot = one_hot_rows(rows, start, CHUNK)
            got = lax.dot_general(back, hot, NT, preferred_element_type=F32)
            own = [returned(i * (CHUNK // BLK) + k) for k in range(CHUNK // BLK)]
            out_ref[:, pl.ds(start, CHUNK)] += got + jnp.concatenate(own, axis=1)

    for half in (0, 1):
        value = hub_part(z, 4 * half, 4, 0)
        for way in (0, 1):
            hops[way, 3, half].wait_recv()
            value = value + arrive[way, 3, half].astype(F32)
        xsum[4 * half : 4 * half + 4] = value
    x_stage[...] = xsum[...].astype(BF)
    rx = [
        go(
            remote(
                x_stage.at[pl.ds(lax.rem(x + o, NX) * HB, HB)],
                x_got.at[o - 1],
                rx_send.at[o - 1],
                rx_recv.at[o - 1],
                device(z, x + o, c, f),
            )
        )
        for o in range(1, NX)
    ]
    y_pass(1)
    for copy in gx:
        copy.wait_recv()
    g_row[...] = g_sum[:, x] + g_x[0] + g_x[1] + g_x[2]
    gz = [
        go(
            remote(
                g_row.at[lax.rem(z + o, NZ)],
                g_z.at[o - 1],
                gz_send.at[o - 1],
                gz_recv.at[o - 1],
                device(z + o, x, c, f),
            )
        )
        for o in range(1, NZ)
    ]
    scatter(0, ROWS_DEV // CHUNK)

    for copy in gz:
        copy.wait_recv()
    done = g_row[z]
    for o in range(1, NZ):
        done = done + g_z[o - 1]
    g_last[...] = done
    move = remote(g_last, g_final, gm_send, gm_recv, swap)

    @pl.when(f != group)
    def _():
        move.start()

    @pl.when(f == group)
    def _():
        g_final[...] = done

    for copy in bz:
        copy.wait_recv()
    value = bsum[z]
    for o in range(1, NZ):
        value = value + bz_got[o - 1].astype(F32)
    sum_ref[:, FD // 2 :] = value
    for copy in rx:
        copy.wait_recv()
    value = xsum[pl.ds(x * HB, HB)]
    for o in range(1, NX):
        value = value + x_got[o - 1].astype(F32)
    sum_ref[:, 0 : FD // 2] = value

    for w in (0, 1):
        y1[w].wait_recv()
        y2[w].wait_recv()
    for half in (0, 1):
        cols = y_cols(half)
        value = mine_ref[0:GR, cols]
        for w in (0, 1):
            value = value + y_last[w, half, 0:GR].astype(F32)
        logits_ref[:, cols] = value.astype(BF)

    @pl.when(f != group)
    def _():
        move.wait()

    score_ref[...] = g_final[...]
    for copy in sent:
        copy.wait_send()


def sage(hub_blocks, tiles, hidden, rows, src, counts, gl, w_self, w_neigh):
    dma = pltpu.SemaphoreType.DMA
    outs = (
        jax.ShapeDtypeStruct((GR, ROWS_DEV), BF),
        jax.ShapeDtypeStruct((8, BLK), F32),
        jax.ShapeDtypeStruct((HB, FD, BLK), F32),
        jax.ShapeDtypeStruct((FD, ROWS_DEV), F32),
    )

    def both(*shape):
        return [dma(shape), dma(shape)]

    return pl.pallas_call(
        sage_kernel,
        out_shape=outs,
        in_specs=[spec(pltpu.SMEM), spec(pl.ANY)] + [spec()] * 7,
        out_specs=(spec(),) * 4,
        scratch_shapes=[
            VM((NB, TPB, BLK, BLK), BF),
            VM((8, POS), jnp.int32),
            pltpu.SMEM((8, POS), jnp.int32),
            VM((EXT, FD, BLK), BF),
            VM((EXT, 16, BLK), BF),
            VM((16, SLOTS), F32),
            VM((NF, GP, ROWS_DEV), BF),
            VM((NF, GP, 2 * FD), BF),
            VM((NF, GP, 2 * FD), BF),
            VM((2 * FD, NF * GP), BF),
            VM((FD, SLOTS), F32),
            VM((NZ, NX, NC, CAP, BLK), BF),
            VM((NZ, NX, CAP, BLK), BF),
            VM((NZ, NX, CAP, BLK), BF),
            VM((NZ, NX, CAP, BLK), BF),
            VM((NX, NZ, CAP, BLK), BF),
            VM((NB, 8, BLK), F32),
            VM((NB + 1, FD, BLK), BF),
            VM((PAIRS, FD, BLK), F32),
            VM((NX, NZ, CAP, BLK), BF),
            VM((PARTS * HB, FD, BLK), BF),
            VM((NF, GP, ROWS_DEV), BF),
            VM((GP, ROWS_DEV), F32),
            VM((NF, GP, WIDE), F32),
            VM((2 * FD, NF * GP), F32),
            VM((NZ, NX, NC, 8, BLK), F32),
            VM((2, GP, HALF), BF),
            VM((2, GP, HALF), BF),
            VM((2, 2, GP, HALF), BF),
            VM((NZ, 8, FD, BLK), BF),
            VM((2, 4, 2, 4, FD // 2, BLK), BF),
            VM((2, 4, 2, 4, FD // 2, BLK), BF),
            VM((8, FD // 2, BLK), BF),
            VM((NX - 1, HB, FD // 2, BLK), BF),
            VM((8, FD // 2, BLK), F32),
            VM((NX - 1, NZ, HB, FD // 2, BLK), BF),
            VM((NX - 1, NZ, HB, FD // 2, BLK), BF),
            VM((NZ, HB, FD // 2, BLK), F32),
            VM((NZ, HB, FD // 2, BLK), BF),
            VM((NZ - 1, HB, FD // 2, BLK), BF),
            VM((NX, NZ, CAP, BLK), BF),
            VM((NZ, NX, CAP, BLK), BF),
            VM((NZ, NX, CAP, BLK), BF),
            VM((NZ, NX, 8, BLK), F32),
            VM((NZ, NX, 8, BLK), F32),
            VM((NX - 1, NZ, 8, BLK), F32),
            VM((NZ, 8, BLK), F32),
            VM((NZ - 1, 8, BLK), F32),
            VM((8, BLK), F32),
            VM((8, BLK), F32),
            dma((LOADS,)),
            dma,
        ]
        + both(2, 3)
        + both(3)
        + both(3)
        + both(2, 4, 2)
        + both(8, 2)
        + [dma, dma]
        + both(7)
        + both(3)
        + both(2, 3)
        + both(8)
        + both(2, 4, 2)
        + both(3)
        + both(3)
        + both(7)
        + both(3)
        + both(7)
        + [dma, dma]
        + [dma, dma]
        + both(3)
        + both(7)
        + [dma, dma],
        compiler_params=pltpu.CompilerParams(
            collective_id=0, has_side_effects=True, vmem_limit_bytes=60 << 20
        ),
    )(hub_blocks, tiles, hidden, rows, src, counts, gl, w_self, w_neigh)


def finish_kernel(hub_ref, out_in, sum_in, logits_in, score_in, logits, gself, gneigh, out):
    out[...] = out_in[...]
    for i in range(HB):
        start = pl.multiple_of(hub_ref[0, i] * BLK, BLK)
        out[:, pl.ds(start, BLK)] += sum_in[i]
    logits[...] = logits_in[...]
    gself[...] = score_in[0:4, 0:GR]
    gneigh[...] = score_in[4:8, 0:GR]


def finish(hub_blocks, out, hub_sum, logits, score):
    outs = (
        jax.ShapeDtypeStruct((GR, ROWS_DEV), BF),
        jax.ShapeDtypeStruct((4, GR), F32),
        jax.ShapeDtypeStruct((4, GR), F32),
        jax.ShapeDtypeStruct((FD, ROWS_DEV), F32),
    )
    return pl.pallas_call(
        finish_kernel,
        out_shape=outs,
        in_specs=[spec(pltpu.SMEM)] + [spec()] * 4,
        out_specs=(spec(),) * 4,
        compiler_params=pltpu.CompilerParams(vmem_limit_bytes=60 << 20),
    )(hub_blocks, out, hub_sum, logits, score)


def local(
    hidden,
    tiles,
    tile_src,
    hub_blocks,
    halo_rows,
    halo_counts,
    weight_self,
    weight_neigh,
    grad_logits,
):
    logits, score, hub_sum, out = sage(
        hub_blocks,
        tiles,
        hidden,
        halo_rows[0].T,
        tile_src.T,
        halo_counts,
        grad_logits,
        weight_self,
        weight_neigh,
    )
    logits, gself, gneigh, out = finish(hub_blocks, out, hub_sum, logits, score)
    return logits, gself.T, gneigh.T, out


def solution(mesh):
    placed = (
        P("feat", "dom"),
        P("dom", None, None, None),
        P("dom", None),
        P("dom", None),
        P("dom", None, None),
        P(),
        P("feat", None),
        P("feat", None),
        P("feat", "dom"),
    )
    return jax.shard_map(
        local,
        mesh=mesh,
        in_specs=placed,
        out_specs=(P("feat", "dom"), P("feat", "dom"), P("feat", "dom"), P("feat", "dom")),
        check_vma=False,
    )
```
